256 devices in a mesh: pp: 8 (over z), ep: 32 (over x, y, core).
Axes of the slice: x: 4, y: 4, z: 8, core: 2. Of those that a mesh axis runs over, the one named last changes fastest.
Arguments:
- fwd_input: bfloat16 [8, 2048, 3584], P('pp', 'ep'), may hold values from -6 to 6
- fwd_experts: int32 [8, 2048, 2], P('pp', 'ep'), may hold values from 0 to 15, all different within a row; in each aligned block of 64 rows (0 to 63, 64 to 127, ..., all dimensions but the last counted through in order) at most 10 rows name the same one
- fwd_gates: float32 [8, 2048, 2], P('pp', 'ep'), may hold values from 0.1 to 1
- bwd_input: bfloat16 [8, 2048, 3584], P('pp', 'ep'), may hold values from -6 to 6
- bwd_cotangent: bfloat16 [8, 2048, 3584], P('pp', 'ep'), may hold values from -6 to 6
- bwd_experts: int32 [8, 2048, 2], P('pp', 'ep'), may hold values from 0 to 15, all different within a row; in each aligned block of 64 rows (0 to 63, 64 to 127, ..., all dimensions but the last counted through in order) at most 10 rows name the same one
- bwd_gates: float32 [8, 2048, 2], P('pp', 'ep'), may hold values from 0.1 to 1
- w_gate: bfloat16 [8, 3584, 16384], P('pp', None, 'ep'), may hold values from -0.09375 to 0.09375
- w_up: bfloat16 [8, 3584, 16384], P('pp', None, 'ep'), may hold values from -0.09375 to 0.09375
- w_down: bfloat16 [8, 16384, 3584], P('pp', 'ep'), may hold values from -0.1875 to 0.1875
Outputs:
- next_input: bfloat16 [8, 2048, 3584], P('pp', 'ep')
- next_cotangent: bfloat16 [8, 2048, 3584], P('pp', 'ep')
The draws below stay inside these ranges and needn't reach their ends.
Inputs may be any that keep to these rules, and one draw needn't show every extreme that they name: `fwd_experts`: A token's 2 experts differ; within each block of 64 consecutive tokens of a layer no expert is chosen more than 10 times. `bwd_experts`: as for fwd_experts.
All inputs are finite; a program needn't handle non-finite values.
Results may differ from the reference program's by a relative error of at most 0.009.
Values may be sent and summed in bfloat16 or wider, within the bound.
A program may use at most 128 MiB of HBM per device.

```python
import math
import jax
import jax.numpy as jnp
import numpy as np
from jax import lax

D = 3584
FF = 1024
GROUP = 2
TOPK = 2
TOK_DEV = 64
EXPERTS = 16
CAP = 10
TOKENS = 2048
N_PP = 8
N_EP = 32


def block_levels(key, dims, split, low, high):
    loudness, own = 1.0, jax.random.fold_in(key, 6)
    for axis_at, blocks in split:
        heights = jnp.exp(jax.random.uniform(jax.random.fold_in(own, axis_at), (blocks,), jnp.float32, low / len(split), high / len(split)))
        loudness = loudness * jnp.repeat(heights, dims[axis_at] // blocks).reshape([-1 if axis == axis_at else 1 for axis in range(len(dims))])
    return loudness


def shared_out(stream_key, own, number, rows, amount, top, most, skew):
    sequence = jax.random.permutation(stream_key, amount)
    packed, usual = portions_of(amount, rows * top, most, skew, True), portions_of(amount, rows * top, most, skew, False)
    places = jnp.arange(amount)

    def named(tallies, offset_by):
        used = int((tallies > 0).sum())
        fixed = max(1, used // 4)
        passed = fixed + (places - fixed + offset_by * (used - fixed)) % max(1, amount - fixed)
        return jnp.zeros((amount,), jnp.int32).at[sequence[jnp.where(places < fixed, places, passed)]].set(jnp.asarray(tallies, jnp.int32))

    tallies = jnp.where(number % 4 == 0, named(packed, number // 4), named(usual, number - number // 4 - 1))
    mixed = jax.random.permutation(jax.random.fold_in(own, 3), amount)
    giver, receiver = mixed[0:amount // 2 * 2:2], mixed[1:amount // 2 * 2:2]
    margin = jnp.minimum(tallies[giver] - 1, most - tallies[receiver]) // 2
    margin = jnp.where((giver == sequence[0]) | (receiver == sequence[0]) | (tallies[receiver] == 0), 0, jnp.maximum(margin, 0))
    passed = jax.random.randint(jax.random.fold_in(own, 4), (amount // 2,), 0, 1 << 20) % (margin + 1)
    tallies = tallies.at[giver].add(-passed).at[receiver].add(passed)
    items = jnp.searchsorted(jnp.cumsum(tallies), jnp.arange(rows * top), side="right").astype(jnp.int32)
    grid = items.reshape(top, rows).T
    grid = grid[jax.random.permutation(jax.random.fold_in(own, 1), rows)]
    offset_by = jax.random.randint(jax.random.fold_in(own, 2), (rows, 1), 0, top)
    return jnp.take_along_axis(grid, (jnp.arange(top)[None, :] + offset_by) % top, axis=1)


def portions_of(amount, total, most, skew, full):
    weights = [(1 << 20) // math.isqrt(rank ** skew) + 1 for rank in range(1, amount + 1)]
    largest = most if full else min(most, max(-(-total // amount), total * weights[0] // sum(weights)))
    least = 1 if total - largest >= amount - 1 else 0
    holding, spare = [largest] + [least] * (amount - 1), total - largest - least * (amount - 1)
    while spare > 0:
        free = [i for i in range(1, amount) if holding[i] < largest] or [i for i in range(1, amount) if holding[i] < most]
        whole, left = sum([weights[i] for i in free]), spare
        for i in free:
            more = min(most - holding[i], max(1, left * weights[i] // whole), spare)
            holding[i] = holding[i] + more
            spare = spare - more
    return np.array(holding)


def normal_values(stream_key, extent, spread, most, pieces=(), held_as=jnp.bfloat16):
    drawn = jax.random.normal(stream_key, extent, jnp.float32) * spread
    if len(pieces) > 0:
        drawn = block_levels(stream_key, extent, pieces, -0.22, 0.18) * drawn
    return jnp.clip(drawn, min=-most, max=most).astype(held_as)


def setup_inputs(seed: int = 0) -> dict:
    key_of = jax.random.split(jax.random.key(seed), 11)
    fwd_input = normal_values(key_of[0], (N_PP, TOKENS, D), 1.0, 6.0, ((0, 8), (1, 32)))
    fwd_experts_keys = jax.random.split(jax.random.fold_in(key_of[1], 1), N_PP * TOKENS // TOK_DEV)
    fwd_experts_turns = jax.random.permutation(jax.random.fold_in(key_of[1], 3), N_PP * TOKENS // TOK_DEV)
    fwd_experts = jax.vmap(lambda own, number: shared_out(jax.random.fold_in(key_of[1], 2), own, number, TOK_DEV, EXPERTS, TOPK, CAP, 2))(fwd_experts_keys, fwd_experts_turns).reshape((N_PP, TOKENS, TOPK))
    fwd_gates = jnp.clip(0.1 + 0.9 * jax.random.uniform(key_of[2], (N_PP, TOKENS, TOPK), jnp.float32) ** block_levels(key_of[2], (N_PP, TOKENS, TOPK), ((0, 8), (1, 32)), -0.2, 0.2), 0.1, 1.0)
    bwd_input = normal_values(key_of[3], (N_PP, TOKENS, D), 1.0, 6.0, ((0, 8), (1, 32)))
    bwd_cotangent = normal_values(key_of[4], (N_PP, TOKENS, D), 1.0, 6.0, ((0, 8), (1, 32)))
    bwd_experts_keys = jax.random.split(jax.random.fold_in(key_of[5], 1), N_PP * TOKENS // TOK_DEV)
    bwd_experts_turns = jax.random.permutation(jax.random.fold_in(key_of[5], 3), N_PP * TOKENS // TOK_DEV)
    bwd_experts = jax.vmap(lambda own, number: shared_out(jax.random.fold_in(key_of[5], 2), own, number, TOK_DEV, EXPERTS, TOPK, CAP, 2))(bwd_experts_keys, bwd_experts_turns).reshape((N_PP, TOKENS, TOPK))
    bwd_gates = jnp.clip(0.1 + 0.9 * jax.random.uniform(key_of[6], (N_PP, TOKENS, TOPK), jnp.float32) ** block_levels(key_of[6], (N_PP, TOKENS, TOPK), ((0, 8), (1, 32)), -0.2, 0.2), 0.1, 1.0)
    w_gate = normal_values(key_of[7], (N_PP, D, EXPERTS * FF), D ** -0.5, 0.09375, ((0, 8), (2, 32)))
    w_up = normal_values(key_of[8], (N_PP, D, EXPERTS * FF), D ** -0.5, 0.09375, ((0, 8), (2, 32)))
    w_down = normal_values(key_of[9], (N_PP, EXPERTS * FF, D), FF ** -0.5, 0.1875, ((0, 8), (1, 32)))
    return dict(fwd_input=fwd_input, fwd_experts=fwd_experts, fwd_gates=fwd_gates, bwd_input=bwd_input, bwd_cotangent=bwd_cotangent, bwd_experts=bwd_experts, bwd_gates=bwd_gates, w_gate=w_gate, w_up=w_up, w_down=w_down)


def pick_rows(expert_ids, gate_vals, expert):
    hits = expert_ids == expert
    chosen = jnp.any(hits, axis=1)
    weight = jnp.sum(jnp.where(hits, gate_vals, 0.0), axis=1)
    limit = N_EP * CAP
    index = jnp.nonzero(chosen, size=limit, fill_value=TOKENS)[0].astype(jnp.int32)
    weight_pad = jnp.concatenate([weight, jnp.zeros((1,), jnp.float32)])
    return index, weight_pad[index]


def section_step(operands):
    fwd_x, fwd_ids, fwd_g, bwd_x, bwd_cot, bwd_ids, bwd_g, gate_all, up_all, down_all = operands
    unit = FF // GROUP
    zero_row = jnp.zeros((1, D), jnp.bfloat16)
    fwd_pad = jnp.concatenate([fwd_x, zero_row])
    bwd_pad = jnp.concatenate([bwd_x, zero_row])
    cot_pad = jnp.concatenate([bwd_cot, zero_row])
    layer_out = fwd_x.astype(jnp.float32)
    layer_grad = bwd_cot.astype(jnp.float32)
    for expert in range(EXPERTS):
        gate_mat = gate_all[:, expert * FF:(expert + 1) * FF]
        up_mat = up_all[:, expert * FF:(expert + 1) * FF]
        down_mat = down_all[expert * FF:(expert + 1) * FF, :]
        down_blocks = down_mat.astype(jnp.float32).reshape(GROUP, unit, D)
        gate_blocks = gate_mat.astype(jnp.float32).reshape(D, GROUP, unit)
        up_blocks = up_mat.astype(jnp.float32).reshape(D, GROUP, unit)

        index, weight = pick_rows(fwd_ids, fwd_g, expert)
        rows_in = fwd_pad[index]
        pre_gate = jnp.dot(rows_in, gate_mat, preferred_element_type=jnp.float32)
        pre_up = jnp.dot(rows_in, up_mat, preferred_element_type=jnp.float32)
        hidden = (jax.nn.silu(pre_gate) * pre_up).astype(jnp.bfloat16)
        hidden_blocks = hidden.astype(jnp.float32).reshape(-1, GROUP, unit)
        parts = jnp.einsum("lgu,gud->lgd", hidden_blocks, down_blocks).astype(jnp.bfloat16)
        summed = jnp.sum(parts.astype(jnp.float32), axis=1)
        layer_out = layer_out.at[index].add(weight[:, None] * summed, mode="drop")

        index_b, weight_b = pick_rows(bwd_ids, bwd_g, expert)
        rows_b = bwd_pad[index_b]
        scaled = (weight_b[:, None] * cot_pad[index_b].astype(jnp.float32)).astype(jnp.bfloat16)
        pre_gate = jnp.dot(rows_b, gate_mat, preferred_element_type=jnp.float32)
        pre_up = jnp.dot(rows_b, up_mat, preferred_element_type=jnp.float32)
        d_hidden = lax.dot_general(scaled, down_mat, (((1,), (1,)), ((), ())), preferred_element_type=jnp.float32)
        sig = jax.nn.sigmoid(pre_gate)
        d_gate = (d_hidden * pre_up * sig * (1.0 + pre_gate * (1.0 - sig))).astype(jnp.bfloat16)
        d_up = (d_hidden * (pre_gate * sig)).astype(jnp.bfloat16)
        d_parts = jnp.einsum("lgu,dgu->lgd", d_gate.astype(jnp.float32).reshape(-1, GROUP, unit), gate_blocks)
        d_parts = d_parts + jnp.einsum("lgu,dgu->lgd", d_up.astype(jnp.float32).reshape(-1, GROUP, unit), up_blocks)
        d_summed = jnp.sum(d_parts.astype(jnp.bfloat16).astype(jnp.float32), axis=1)
        layer_grad = layer_grad.at[index_b].add(d_summed, mode="drop")
    return layer_out.astype(jnp.bfloat16), layer_grad.astype(jnp.bfloat16)


def reference(fwd_input, fwd_experts, fwd_gates, bwd_input, bwd_cotangent, bwd_experts, bwd_gates, w_gate, w_up, w_down):
    layer_out, layer_grad = lax.map(section_step, (fwd_input, fwd_experts, fwd_gates, bwd_input, bwd_cotangent, bwd_experts, bwd_gates, w_gate, w_up, w_down))
    return jnp.roll(layer_out, 1, axis=0), jnp.roll(layer_grad, -1, axis=0)
```

```python
import jax
import jax.numpy as jnp
from jax import lax
from jax.experimental import pallas as pl
from jax.experimental.pallas import tpu as pltpu
from jax.sharding import PartitionSpec as P

MESH = pl.DeviceIdType.MESH
F32 = jnp.float32
BF16 = jnp.bfloat16

D = 3584
UNIT = 512
TOK = 64
CHIPS = 16
SIDE = 4
ROWS = 160
HALF = D // 2
PIECE = 512
PIECES = D // PIECE
WIDE = HALF + PIECE
MSG = CHIPS * 16
BLOCK = 256


def dot(a, b):
    return lax.dot_general(a, b, (((1,), (0,)), ((), ())), preferred_element_type=F32)


def dot_nt(a, b):
    return lax.dot_general(a, b, (((1,), (1,)), ((), ())), preferred_element_type=F32)


def iota(shape, dim):
    return lax.broadcasted_iota(jnp.int32, shape, dim)


def as_hot(mask):
    return jnp.where(mask, 1.0, 0.0).astype(BF16)


def routing(ids):
    expert = iota((CHIPS, TOK), 0)
    first, second = ids[0:1, :] == expert, ids[1:2, :] == expert
    hits = jnp.where(first | second, 1.0, 0.0)
    before = as_hot(iota((TOK, TOK), 0) < iota((TOK, TOK), 1))
    keys = hits * (dot(hits.astype(BF16), before) + 1.0)
    copies = as_hot((iota((TOK, 9 * TOK), 1) & (TOK - 1)) == iota((TOK, 9 * TOK), 0))
    wide = dot(keys.astype(BF16), copies).astype(BF16)
    key = dot(rows_of_expert(BF16), wide)
    slot = (iota((MSG, 9 * TOK), 0) & 15).astype(F32)
    piece = iota((MSG, 9 * TOK), 1) >> 6
    want_main = slot - 8.0 * piece.astype(F32)
    want_rest = slot - 2.0 * (piece - 2).astype(F32)
    main = (want_main >= 0.0) & (want_main < 8.0) & (key == want_main + 1.0)
    rest = (want_rest >= 0.0) & (want_rest < 2.0) & (key == want_rest + 9.0)
    hot = as_hot(main | rest)
    return key[:, :TOK], hot, first, second


def rows_of_expert(dtype):
    row, expert = iota((MSG, CHIPS), 0), iota((MSG, CHIPS), 1)
    return jnp.where((row >> 4) == expert, 1.0, 0.0).astype(dtype)


def slot_gates(key, first, second, gates):
    per = jnp.where(first, gates[0:1, :], 0.0) + jnp.where(second, gates[1:2, :], 0.0)
    spread = lax.dot_general(
        rows_of_expert(F32),
        per,
        (((1,), (0,)), ((), ())),
        precision=lax.Precision.HIGHEST,
        preferred_element_type=F32,
    )
    slot = iota((MSG, TOK), 0)
    main = key == (slot & 7).astype(F32) + 1.0
    rest = key == (slot & 1).astype(F32) + 9.0
    return (
        jnp.sum(jnp.where(main, spread, 0.0), axis=1, keepdims=True),
        jnp.sum(jnp.where(rest, spread, 0.0), axis=1, keepdims=True),
    )


def place(u, v):
    return (((u >> 1) & 15) << 4) + ((u >> 5) << 1) + (u & 1) == v


def kernel(
    fids, fgates, bids, bgates, xf, xb, cb, gate, up, down,
    out_f, out_b,
    half_x, piece_x, send_b, send_f, recv_b, recv_f, ret_b, ret_f, got_b, got_f,
    wg, wu, wd, rows_v, rows_s, act_a, act_b, rest_z, next_x, next_c,
    n_fids, n_fgates, n_bids, hot_m, hot_r,
    in_sem, w_sem, own_sem, wx_send, wx_recv, z_send, z_recv,
    sb_sem, rb_sem, sf_sem, rf_sem, tb_send, tb_recv, tf_send, tf_recv, ready,
):
    z, me = lax.axis_index("pp"), lax.axis_index("ep")
    sections = lax.axis_size("pp")
    chip, core = me // 2, lax.rem(me, 2)
    above, below = lax.rem(z + 1, sections), lax.rem(z + sections - 1, sections)
    sibling = chip * 2 + 1 - core

    def peer(k):
        x = lax.rem(chip // SIDE + k // SIDE, SIDE)
        y = lax.rem(lax.rem(chip, SIDE) + lax.rem(k, SIDE), SIDE)
        return x * SIDE + y

    barrier = pltpu.get_barrier_semaphore()

    def greet(k, carry):
        pl.semaphore_signal(
            barrier, inc=1, device_id=(z, peer(k) * 2 + core), device_id_type=MESH
        )
        return carry

    lax.fori_loop(1, CHIPS, greet, 0)
    for target in ((z, sibling), (above, me), (below, me)):
        pl.semaphore_signal(barrier, inc=1, device_id=target, device_id_type=MESH)

    loads = []
    for i, src in enumerate((xb, cb, xf)):
        own = []
        for h in range(2):
            own.append(
                pltpu.make_async_copy(
                    src.at[:, pl.ds(h * HALF, HALF)],
                    half_x.at[i, pl.ds(h * TOK, TOK)],
                    in_sem.at[i * 9 + h],
                )
            )
        for k in range(PIECES):
            own.append(
                pltpu.make_async_copy(
                    src.at[:, pl.ds(k * PIECE, PIECE)],
                    piece_x.at[i, pl.ds(k * TOK, TOK)],
                    in_sem.at[i * 9 + 2 + k],
                )
            )
        for copy in own:
            copy.start()
        loads.append(own)
    weights = [
        pltpu.make_async_copy(src, dst.at[0], w_sem.at[i])
        for i, (src, dst) in enumerate(((gate, wg), (up, wu), (down, wd)))
    ]

    def message(i, hot, scales):
        main = dot(hot[:, : 2 * TOK], half_x[i])
        rest = dot(hot[:, 2 * TOK :], piece_x[i])
        if scales is not None:
            main, rest = main * scales[0], rest * scales[1]
        return (
            main.astype(BF16).reshape(CHIPS, 16, HALF),
            rest.astype(BF16).reshape(CHIPS, 16, PIECE),
        )

    key_b, hot_b, first_b, second_b = routing(bids[...])
    scales_b = slot_gates(key_b, first_b, second_b, bgates[...])
    for i in range(2):
        for copy in loads[i]:
            copy.wait()
        main, rest = message(i, hot_b, None if i == 0 else scales_b)
        send_b[:, i, :, :HALF] = main
        send_b[:, i, :, HALF:] = rest

    pl.semaphore_wait(barrier, CHIPS - 1 + 3)

    def to_expert(k, src, dst, send_sem, recv_sem):
        q = peer(k)
        return pltpu.make_async_remote_copy(
            src_ref=src.at[q],
            dst_ref=dst.at[chip],
            send_sem=send_sem.at[k],
            recv_sem=recv_sem.at[k],
            device_id=(z, q * 2 + core),
            device_id_type=MESH,
        )

    def expert_b(k):
        return to_expert(k, send_b, recv_b, sb_sem, rb_sem)

    def expert_f(k):
        return to_expert(k, send_f, recv_f, sf_sem, rf_sem)

    def start_b(k, carry):
        expert_b(k).start()
        return carry

    lax.fori_loop(1, CHIPS, start_b, 0)
    own_b = pltpu.make_async_copy(send_b.at[chip], recv_b.at[chip], own_sem.at[0])
    own_b.start()
    exchange = [
        pltpu.make_async_remote_copy(
            src_ref=src,
            dst_ref=dst.at[1],
            send_sem=wx_send.at[i],
            recv_sem=wx_recv.at[i],
            device_id=(z, sibling),
            device_id_type=MESH,
        )
        for i, (src, dst) in enumerate(((gate, wg), (up, wu), (down, wd)))
    ]
    for copy in weights:
        copy.start()
    for copy in exchange:
        copy.start()
    vertical = [
        pltpu.make_async_remote_copy(
            src_ref=src,
            dst_ref=dst,
            send_sem=z_send.at[i],
            recv_sem=z_recv.at[i],
            device_id=(section, me),
            device_id_type=MESH,
        )
        for i, (src, dst, section) in enumerate(
            (
                (xf, next_x, above),
                (fids, n_fids, above),
                (fgates, n_fgates, above),
                (cb, next_c, below),
                (bids, n_bids, below),
            )
        )
    ]
    for copy in vertical:
        copy.start()

    _, hot_f, _, _ = routing(fids[...])
    for copy in loads[2]:
        copy.wait()
    main, rest = message(2, hot_f, None)
    send_f[:, :, :HALF] = main
    send_f[:, :, HALF:] = rest

    def start_f(k, carry):
        expert_b(k).wait_send()
        expert_f(k).start()
        return carry

    lax.fori_loop(1, CHIPS, start_f, 0)
    own_f = pltpu.make_async_copy(send_f.at[chip], recv_f.at[chip], own_sem.at[1])
    own_f.start()

    def flip(hot):
        n = hot.shape[1]
        unit = as_hot(iota((n, n), 0) == iota((n, n), 1))
        return dot_nt(unit, hot).astype(BF16)

    for i in (1, 2, 4):
        vertical[i].wait_recv()
    _, hot, _, _ = routing(n_bids[...])
    hot_m[0] = flip(hot[:, : 2 * TOK])
    hot_r[0] = flip(hot[:, 2 * TOK :])
    key, hot, first, second = routing(n_fids[...])
    scale_m, scale_r = slot_gates(key, first, second, n_fgates[...])
    high_m, high_r = scale_m.astype(BF16).astype(F32), scale_r.astype(BF16).astype(F32)
    hot_main, hot_rest = hot[:, : 2 * TOK].astype(F32), hot[:, 2 * TOK :].astype(F32)
    hot_m[1] = flip((hot_main * high_m).astype(BF16))
    hot_r[1] = flip((hot_rest * high_r).astype(BF16))
    hot_m[2] = flip((hot_main * (scale_m - high_m)).astype(BF16))
    hot_r[2] = flip((hot_rest * (scale_r - high_r)).astype(BF16))

    def unpack(load, dst):
        def step(i, carry):
            pair = load(pl.ds(2 * i, 2), pl.ds(0, HALF)).astype(F32)
            halves = pair.reshape(2, 2, 8, HALF)
            rows = pl.ds(pl.multiple_of(16 * i, 16), 16)
            dst[rows, :HALF] = halves[:, 0].reshape(16, HALF).astype(BF16)
            dst[rows, HALF:] = halves[:, 1].reshape(16, HALF).astype(BF16)
            return carry

        lax.fori_loop(0, CHIPS // 2, step, 0)
        rest = load(pl.ds(0, CHIPS), pl.ds(HALF, PIECE)).reshape(MSG, PIECE)
        n = PIECES * 32
        order = as_hot(place(iota((n, MSG), 0), iota((n, MSG), 1)))
        plain = dot(order, rest).astype(BF16)
        for k in range(PIECES):
            dst[128:ROWS, k * PIECE : (k + 1) * PIECE] = plain[32 * k : 32 * k + 32]

    def pack(column, dst):
        def keep(c, rows):
            rest_z[
                pl.ds(pl.multiple_of((c // 2) * 32, 32), 32),
                pl.ds(pl.multiple_of(lax.rem(c, 2) * BLOCK, BLOCK), BLOCK),
            ] = rows.astype(BF16)

        def step(n, carry):
            low, high = column(n), column(n + 7)
            main = jnp.concatenate(
                [low[:128].reshape(CHIPS, 8, BLOCK), high[:128].reshape(CHIPS, 8, BLOCK)], axis=1
            )
            dst[:, :, pl.ds(pl.multiple_of(n * BLOCK, BLOCK), BLOCK)] = main.astype(BF16)
            keep(n, low[128:])
            keep(n + 7, high[128:])
            return carry

        lax.fori_loop(0, HALF // BLOCK, step, 0)
        n = PIECES * 32
        order = as_hot(place(iota((MSG, n), 1), iota((MSG, n), 0)))
        dst[:, :, HALF:] = dot(order, rest_z[...]).astype(BF16).reshape(CHIPS, 16, PIECE)

    def unit_of(u):
        return u // 2, pl.ds(pl.multiple_of(lax.rem(u, 2) * BLOCK, BLOCK), BLOCK)

    def act_of(u):
        return pl.ds(pl.multiple_of(u * BLOCK, BLOCK), BLOCK)

    def arrive_b(k, carry):
        expert_b(k).wait_recv()
        return carry

    lax.fori_loop(1, CHIPS, arrive_b, 0)
    own_b.wait()
    pl.semaphore_signal(ready.at[0], inc=1, device_id=(above, me), device_id_type=MESH)
    pl.semaphore_signal(ready.at[1], inc=1, device_id=(below, me), device_id_type=MESH)
    unpack(lambda i, j: recv_b[i, 0, :, j], rows_v)
    unpack(lambda i, j: recv_b[i, 1, :, j], rows_s)
    for copy in weights:
        copy.wait()

    def hidden_b(u, carry):
        j, cols = unit_of(u)
        a = dot(rows_v[...], wg[j, :, cols])
        b = dot(rows_v[...], wu[j, :, cols])
        dh = dot_nt(rows_s[...], wd[j, cols, :])
        sig = jax.nn.sigmoid(a)
        act_a[:, act_of(u)] = (dh * b * sig * (1.0 + a * (1.0 - sig))).astype(BF16)
        act_b[:, act_of(u)] = (dh * (a * sig)).astype(BF16)
        return carry

    lax.fori_loop(0, 2, hidden_b, 0)
    for copy in exchange:
        copy.wait_recv()
    lax.fori_loop(2, 4, hidden_b, 0)

    def column_b(n):
        rows = pl.ds(pl.multiple_of(n * BLOCK, BLOCK), BLOCK)
        total = jnp.zeros((ROWS, BLOCK), F32)
        for j in range(2):
            total += dot_nt(act_a[:, j * UNIT : (j + 1) * UNIT], wg[j, rows, :])
            total += dot_nt(act_b[:, j * UNIT : (j + 1) * UNIT], wu[j, rows, :])
        return total

    pack(column_b, ret_b)

    def to_token(k, section, src, dst, send_sem, recv_sem):
        q = peer(k)
        return pltpu.make_async_remote_copy(
            src_ref=src.at[q],
            dst_ref=dst.at[chip],
            send_sem=send_sem.at[k],
            recv_sem=recv_sem.at[k],
            device_id=(section, q * 2 + core),
            device_id_type=MESH,
        )

    def token_b(k):
        return to_token(k, below, ret_b, got_b, tb_send, tb_recv)

    def token_f(k):
        return to_token(k, above, ret_f, got_f, tf_send, tf_recv)

    pl.semaphore_wait(ready.at[0], 1)

    def return_b(k, carry):
        token_b(k).start()
        return carry

    lax.fori_loop(0, CHIPS, return_b, 0)

    def arrive_f(k, carry):
        expert_f(k).wait_recv()
        return carry

    lax.fori_loop(1, CHIPS, arrive_f, 0)
    own_f.wait()
    unpack(lambda i, j: recv_f[i, :, j], rows_v)

    def hidden_f(u, carry):
        j, cols = unit_of(u)
        a = dot(rows_v[...], wg[j, :, cols])
        b = dot(rows_v[...], wu[j, :, cols])
        act_a[:, act_of(u)] = (a * jax.nn.sigmoid(a) * b).astype(BF16)
        return carry

    lax.fori_loop(0, 4, hidden_f, 0)

    def column_f(n):
        cols = pl.ds(pl.multiple_of(n * BLOCK, BLOCK), BLOCK)
        total = jnp.zeros((ROWS, BLOCK), F32)
        for j in range(2):
            total += dot(act_a[:, j * UNIT : (j + 1) * UNIT], wd[j, :, cols])
        return total

    pack(column_f, ret_f)
    pl.semaphore_wait(ready.at[1], 1)

    def return_f(k, carry):
        token_f(k).start()
        return carry

    lax.fori_loop(0, CHIPS, return_f, 0)

    def combine(got, kinds, base, out):
        main = sum(dot(hot_m[i], got[:, :, :HALF].reshape(MSG, HALF)) for i in kinds)
        rest = sum(dot(hot_r[i], got[:, :, HALF:].reshape(MSG, PIECE)) for i in kinds)
        for c in range(2 * HALF // BLOCK):
            h, at = c // 7, (c % 7) * BLOCK
            k, off = c // 2, (c % 2) * BLOCK
            cols = slice(c * BLOCK, (c + 1) * BLOCK)
            out[:, cols] = (
                base[:, cols].astype(F32)
                + main[h * TOK : (h + 1) * TOK, at : at + BLOCK]
                + rest[k * TOK : (k + 1) * TOK, off : off + BLOCK]
            ).astype(BF16)

    for i in (0, 3):
        vertical[i].wait_recv()

    def back_b(k, carry):
        token_b(k).wait_recv()
        return carry

    def back_f(k, carry):
        token_f(k).wait_recv()
        return carry

    lax.fori_loop(0, CHIPS, back_b, 0)
    combine(got_b, (0,), next_c, out_b)
    lax.fori_loop(0, CHIPS, back_f, 0)
    combine(got_f, (1, 2), next_x, out_f)

    def sent(k, carry):
        token_b(k).wait_send()
        token_f(k).wait_send()
        return carry

    def sent_f(k, carry):
        expert_f(k).wait_send()
        return carry

    lax.fori_loop(1, CHIPS, sent_f, 0)
    lax.fori_loop(0, CHIPS, sent, 0)
    for copy in exchange + vertical:
        copy.wait_send()


def body(
    fwd_input, fwd_experts, fwd_gates, bwd_input, bwd_cotangent, bwd_experts, bwd_gates,
    w_gate, w_up, w_down,
):
    vmem, anywhere = pl.BlockSpec(memory_space=pltpu.VMEM), pl.BlockSpec(memory_space=pl.ANY)
    token_rows = jax.ShapeDtypeStruct((TOK, D), BF16)
    messages = pltpu.VMEM((CHIPS, 16, WIDE), BF16)
    pairs = pltpu.VMEM((CHIPS, 2, 16, WIDE), BF16)
    sixteen = pltpu.SemaphoreType.DMA((CHIPS,))
    out_f, out_b = pl.pallas_call(
        kernel,
        out_shape=(token_rows, token_rows),
        in_specs=[vmem] * 4 + [anywhere] * 6,
        out_specs=(vmem, vmem),
        scratch_shapes=[
            pltpu.VMEM((3, 2 * TOK, HALF), BF16),
            pltpu.VMEM((3, PIECES * TOK, PIECE), BF16),
            pairs, messages, pairs, messages, messages, messages, messages, messages,
            pltpu.VMEM((2, D, UNIT), BF16),
            pltpu.VMEM((2, D, UNIT), BF16),
            pltpu.VMEM((2, UNIT, D), BF16),
            pltpu.VMEM((ROWS, D), BF16),
            pltpu.VMEM((ROWS, D), BF16),
            pltpu.VMEM((ROWS, 2 * UNIT), BF16),
            pltpu.VMEM((ROWS, 2 * UNIT), BF16),
            pltpu.VMEM((PIECES * 32, PIECE), BF16),
            pltpu.VMEM((TOK, D), BF16),
            pltpu.VMEM((TOK, D), BF16),
            pltpu.VMEM((2, TOK), jnp.int32),
            pltpu.VMEM((2, TOK), F32),
            pltpu.VMEM((2, TOK), jnp.int32),
            pltpu.VMEM((3, 2 * TOK, MSG), BF16),
            pltpu.VMEM((3, PIECES * TOK, MSG), BF16),
            pltpu.SemaphoreType.DMA((27,)),
            pltpu.SemaphoreType.DMA((3,)),
            pltpu.SemaphoreType.DMA((2,)),
            pltpu.SemaphoreType.DMA((3,)),
            pltpu.SemaphoreType.DMA((3,)),
            pltpu.SemaphoreType.DMA((5,)),
            pltpu.SemaphoreType.DMA((5,)),
            sixteen, sixteen, sixteen, sixteen, sixteen, sixteen, sixteen, sixteen,
            pltpu.SemaphoreType.REGULAR((2,)),
        ],
        compiler_params=pltpu.CompilerParams(
            collective_id=0, has_side_effects=True, vmem_limit_bytes=60 << 20
        ),
        name="relay_experts",
    )(
        fwd_experts[0].T, fwd_gates[0].T, bwd_experts[0].T, bwd_gates[0].T,
        fwd_input[0], bwd_input[0], bwd_cotangent[0], w_gate[0], w_up[0], w_down[0],
    )
    return out_f[None], out_b[None]


def solution(mesh):
    tokens = P("pp", "ep", None)
    in_specs = (tokens,) * 7 + (P("pp", None, "ep"), P("pp", None, "ep"), tokens)
    return jax.shard_map(
        body, mesh=mesh, in_specs=in_specs, out_specs=(tokens, tokens), check_vma=False
    )
```

```python
import jax
import jax.numpy as jnp
from jax import lax
from jax.experimental import pallas as pl
from jax.experimental.pallas import tpu as pltpu
from jax.sharding import PartitionSpec as P

MESH = pl.DeviceIdType.MESH
F32 = jnp.float32
BF16 = jnp.bfloat16

D = 3584
UNIT = 512
TOK = 64
CHIPS = 16
SIDE = 4
ROWS = 160
HALF = D // 2
PIECE = 512
PIECES = D // PIECE
WIDE = HALF + PIECE
MSG = CHIPS * 16
BLOCK = 256
LANES = 128
CHUNKS = 4
CHUNK = 2 * BLOCK + LANES
HOTS = 10 * TOK
FAR_FIRST = (10, 9, 14, 11, 6, 5, 13, 15, 7, 8, 2, 4, 1, 12, 3)


def dot(a, b):
    return lax.dot_general(a, b, (((1,), (0,)), ((), ())), preferred_element_type=F32)


def dot_nt(a, b):
    return lax.dot_general(a, b, (((1,), (1,)), ((), ())), preferred_element_type=F32)


def iota(shape, dim):
    return lax.broadcasted_iota(jnp.int32, shape, dim)


def as_hot(mask):
    return jnp.where(mask, 1.0, 0.0).astype(BF16)


def routing(ids):
    expert = iota((CHIPS, TOK), 0)
    first, second = ids[0:1, :] == expert, ids[1:2, :] == expert
    hits = jnp.where(first | second, 1.0, 0.0)
    before = as_hot(iota((TOK, TOK), 0) < iota((TOK, TOK), 1))
    keys = hits * (dot(hits.astype(BF16), before) + 1.0)
    copies = as_hot((iota((TOK, HOTS), 1) & (TOK - 1)) == iota((TOK, HOTS), 0))
    wide = dot(keys.astype(BF16), copies).astype(BF16)
    key = dot(rows_of_expert(BF16), wide)
    slot = (iota((MSG, HOTS), 0) & 15).astype(F32)
    piece = iota((MSG, HOTS), 1) >> 6
    want_main = slot - 8.0 * piece.astype(F32)
    want_rest = slot - 2.0 * (piece - 2).astype(F32)
    main = (want_main >= 0.0) & (want_main < 8.0) & (key == want_main + 1.0)
    rest = (want_rest >= 0.0) & (want_rest < 2.0) & (key == want_rest + 9.0)
    hot = as_hot(main | rest)
    return key[:, :TOK], hot, first, second


def rows_of_expert(dtype):
    row, expert = iota((MSG, CHIPS), 0), iota((MSG, CHIPS), 1)
    return jnp.where((row >> 4) == expert, 1.0, 0.0).astype(dtype)


def slot_gates(key, first, second, gates):
    per = jnp.where(first, gates[0:1, :], 0.0) + jnp.where(second, gates[1:2, :], 0.0)
    spread = lax.dot_general(
        rows_of_expert(F32),
        per,
        (((1,), (0,)), ((), ())),
        precision=lax.Precision.HIGHEST,
        preferred_element_type=F32,
    )
    slot = iota((MSG, TOK), 0)
    main = key == (slot & 7).astype(F32) + 1.0
    rest = key == (slot & 1).astype(F32) + 9.0
    return (
        jnp.sum(jnp.where(main, spread, 0.0), axis=1, keepdims=True),
        jnp.sum(jnp.where(rest, spread, 0.0), axis=1, keepdims=True),
    )


def place(u, v):
    return (((u >> 1) & 15) << 4) + ((u >> 5) << 1) + (u & 1) == v


def kernel(
    fids, fgates, bids, bgates, xf, xb, cb, gate, up, down,
    out_f, out_b,
    half_x, piece_x, send_v, send_s, send_f, recv_v, recv_s, recv_f, ret_b, ret_f, got_b, got_f,
    wg, wu, wd, rows_v, rows_s, act_a, act_b, base_x, base_c, sum_f, sum_b, hot_m, hot_r,
    in_sem, base_sem, w_sem, own_sem, wx_send, wx_recv,
    sv_sem, rv_sem, ss_sem, rs_sem, sf_sem, rf_sem,
    tb_send, tb_recv, tf_send, tf_recv, hb_send, hb_recv, hf_send, hf_recv,
):
    z, me = lax.axis_index("pp"), lax.axis_index("ep")
    sections = lax.axis_size("pp")
    chip, core = me // 2, lax.rem(me, 2)
    above, below = lax.rem(z + 1, sections), lax.rem(z + sections - 1, sections)
    sibling = chip * 2 + 1 - core

    def peer(k):
        x = lax.rem(chip // SIDE + k // SIDE, SIDE)
        y = lax.rem(lax.rem(chip, SIDE) + k % SIDE, SIDE)
        return x * SIDE + y

    barrier = pltpu.get_barrier_semaphore()
    for k in FAR_FIRST:
        pl.semaphore_signal(
            barrier, inc=1, device_id=(z, peer(k) * 2 + core), device_id_type=MESH
        )
    for target in ((z, sibling), (above, me), (below, me)):
        pl.semaphore_signal(barrier, inc=1, device_id=target, device_id_type=MESH)

    loads = []
    for i, src in enumerate((xb, cb, xf)):
        own = []
        for h in range(2):
            own.append(
                pltpu.make_async_copy(
                    src.at[:, pl.ds(h * HALF, HALF)],
                    half_x.at[i, pl.ds(h * TOK, TOK)],
                    in_sem.at[i * 9 + h],
                )
            )
        for k in range(PIECES):
            own.append(
                pltpu.make_async_copy(
                    src.at[:, pl.ds(k * PIECE, PIECE)],
                    piece_x.at[i, pl.ds(k * TOK, TOK)],
                    in_sem.at[i * 9 + 2 + k],
                )
            )
        for copy in own:
            copy.start()
        loads.append(own)
    weights = [
        pltpu.make_async_copy(src, dst.at[0], w_sem.at[i])
        for i, (src, dst) in enumerate(((gate, wg), (up, wu), (down, wd)))
    ]
    bases = [
        pltpu.make_async_copy(xf, base_x, base_sem.at[0]),
        pltpu.make_async_copy(cb, base_c, base_sem.at[1]),
    ]

    def message(i, hot, scales, dst):
        for copy in loads[i]:
            copy.wait()
        main = dot(hot[:, : 2 * TOK], half_x[i])
        rest = dot(hot[:, 2 * TOK : 2 * TOK + PIECES * TOK], piece_x[i])
        if scales is not None:
            main, rest = main * scales[0], rest * scales[1]
        dst[:, :, :HALF] = main.astype(BF16).reshape(CHIPS, 16, HALF)
        dst[:, :, HALF:] = rest.astype(BF16).reshape(CHIPS, 16, PIECE)

    def to_expert(k, src, dst, send_sem, recv_sem):
        q = peer(k)
        return pltpu.make_async_remote_copy(
            src_ref=src.at[q],
            dst_ref=dst.at[chip],
            send_sem=send_sem.at[k],
            recv_sem=recv_sem.at[k],
            device_id=(z, q * 2 + core),
            device_id_type=MESH,
        )

    def expert_v(k):
        return to_expert(k, send_v, recv_v, sv_sem, rv_sem)

    def expert_s(k):
        return to_expert(k, send_s, recv_s, ss_sem, rs_sem)

    def expert_f(k):
        return to_expert(k, send_f, recv_f, sf_sem, rf_sem)

    keep_v, keep_s, keep_f = (
        pltpu.make_async_copy(src.at[chip], dst.at[chip], own_sem.at[i])
        for i, (src, dst) in enumerate(((send_v, recv_v), (send_s, recv_s), (send_f, recv_f)))
    )

    key_b, hot_b, first_b, second_b = routing(bids[...])
    message(0, hot_b, None, send_v)
    pl.semaphore_wait(barrier, CHIPS - 1 + 3)
    for k in FAR_FIRST:
        expert_v(k).start()
    keep_v.start()
    message(1, hot_b, slot_gates(key_b, first_b, second_b, bgates[...]), send_s)
    for k in FAR_FIRST:
        expert_s(k).start()
    keep_s.start()

    exchange = [
        pltpu.make_async_remote_copy(
            src_ref=src,
            dst_ref=dst.at[1],
            send_sem=wx_send.at[i],
            recv_sem=wx_recv.at[i],
            device_id=(z, sibling),
            device_id_type=MESH,
        )
        for i, (src, dst) in enumerate(((gate, wg), (up, wu), (down, wd)))
    ]
    for copy in weights + exchange + bases:
        copy.start()

    key_f, hot_f, first_f, second_f = routing(fids[...])
    message(2, hot_f, None, send_f)
    for k in FAR_FIRST:
        expert_s(k).wait_send()
        expert_f(k).start()
    keep_f.start()

    def flip(hot):
        n = hot.shape[1]
        unit = as_hot(iota((n, n), 0) == iota((n, n), 1))
        return dot_nt(unit, hot).astype(BF16)

    hot_m[0] = flip(hot_b[:, : 2 * TOK])
    hot_r[0] = flip(hot_b[:, 2 * TOK :])
    scale_m, scale_r = slot_gates(key_f, first_f, second_f, fgates[...])
    high_m, high_r = scale_m.astype(BF16).astype(F32), scale_r.astype(BF16).astype(F32)
    hot_main, hot_rest = hot_f[:, : 2 * TOK].astype(F32), hot_f[:, 2 * TOK :].astype(F32)
    hot_m[1] = flip((hot_main * high_m).astype(BF16))
    hot_r[1] = flip((hot_rest * high_r).astype(BF16))
    hot_m[2] = flip((hot_main * (scale_m - high_m)).astype(BF16))
    hot_r[2] = flip((hot_rest * (scale_r - high_r)).astype(BF16))

    def unpack(src, dst):
        def step(i, carry):
            pair = src[pl.ds(2 * i, 2), :, :HALF].astype(F32)
            halves = pair.reshape(2, 2, 8, HALF)
            rows = pl.ds(pl.multiple_of(16 * i, 16), 16)
            dst[rows, :HALF] = halves[:, 0].reshape(16, HALF).astype(BF16)
            dst[rows, HALF:] = halves[:, 1].reshape(16, HALF).astype(BF16)
            return carry

        lax.fori_loop(0, CHIPS // 2, step, 0)
        rest = src[:, :, HALF:].reshape(MSG, PIECE)
        n = PIECES * 32
        order = as_hot(place(iota((n, MSG), 0), iota((n, MSG), 1)))
        plain = dot(order, rest).astype(BF16)
        for k in range(PIECES):
            dst[128:ROWS, k * PIECE : (k + 1) * PIECE] = plain[32 * k : 32 * k + 32]

    def unit_of(u):
        return u // 2, pl.ds(pl.multiple_of(lax.rem(u, 2) * BLOCK, BLOCK), BLOCK)

    def act_of(u):
        return pl.ds(pl.multiple_of(u * BLOCK, BLOCK), BLOCK)

    def to_token(k, c, width, src, dst, send_sem, recv_sem):
        q = peer(k)
        return pltpu.make_async_remote_copy(
            src_ref=src.at[c, q, :, pl.ds(0, width)],
            dst_ref=dst.at[c, chip, :, pl.ds(0, width)],
            send_sem=send_sem.at[c],
            recv_sem=recv_sem.at[c],
            device_id=(z, q * 2 + core),
            device_id_type=MESH,
        )

    def emit(column, c, steps, ret, got, send_sem, recv_sem):
        lows = [column(2 * c + i) for i in range(steps)]
        highs = [column(2 * c + i + 7) for i in range(steps)]
        for i in range(steps):
            main = jnp.concatenate(
                [y[:128].reshape(CHIPS, 8, BLOCK) for y in (lows[i], highs[i])], axis=1
            )
            ret[c, :, :, i * BLOCK : (i + 1) * BLOCK] = main.astype(BF16)
        rests = [
            y[128:, j * LANES : (j + 1) * LANES] for y in lows + highs for j in range(BLOCK // LANES)
        ]
        n = len(rests) * 32
        order = as_hot(place(iota((MSG, n), 1), iota((MSG, n), 0)))
        rest = dot(order, jnp.concatenate(rests, axis=0).astype(BF16))
        wide = steps * BLOCK
        ret[c, :, :, wide : wide + LANES] = rest.astype(BF16).reshape(CHIPS, 16, LANES)
        for k in FAR_FIRST:
            to_token(k, c, wide + LANES, ret, got, send_sem, recv_sem).start()
        pltpu.make_async_copy(
            ret.at[c, chip, :, pl.ds(0, wide + LANES)],
            got.at[c, chip, :, pl.ds(0, wide + LANES)],
            recv_sem.at[c],
        ).start()

    def emit_all(column, ret, got, send_sem, recv_sem):
        def step(c, carry):
            emit(column, c, 2, ret, got, send_sem, recv_sem)
            return carry

        lax.fori_loop(0, CHUNKS - 1, step, 0)
        emit(column, CHUNKS - 1, 1, ret, got, send_sem, recv_sem)

    for k in FAR_FIRST:
        expert_v(k).wait_recv()
    keep_v.wait()
    unpack(recv_v, rows_v)
    for k in FAR_FIRST:
        expert_s(k).wait_recv()
    keep_s.wait()
    unpack(recv_s, rows_s)
    for copy in weights:
        copy.wait()

    def hidden_b(u, carry):
        j, cols = unit_of(u)
        a = dot(rows_v[...], wg[j, :, cols])
        b = dot(rows_v[...], wu[j, :, cols])
        dh = dot_nt(rows_s[...], wd[j, cols, :])
        sig = jax.nn.sigmoid(a)
        act_a[:, act_of(u)] = (dh * b * sig * (1.0 + a * (1.0 - sig))).astype(BF16)
        act_b[:, act_of(u)] = (dh * (a * sig)).astype(BF16)
        return carry

    lax.fori_loop(0, 2, hidden_b, 0)
    for copy in exchange:
        copy.wait_recv()
    lax.fori_loop(2, 4, hidden_b, 0)

    def column_b(n):
        rows = pl.ds(pl.multiple_of(n * BLOCK, BLOCK), BLOCK)
        total = jnp.zeros((ROWS, BLOCK), F32)
        for j in range(2):
            total += dot_nt(act_a[:, j * UNIT : (j + 1) * UNIT], wg[j, rows, :])
            total += dot_nt(act_b[:, j * UNIT : (j + 1) * UNIT], wu[j, rows, :])
        return total

    emit_all(column_b, ret_b, got_b, tb_send, tb_recv)

    for k in FAR_FIRST:
        expert_f(k).wait_recv()
    keep_f.wait()
    unpack(recv_f, rows_v)

    def hidden_f(u, carry):
        j, cols = unit_of(u)
        a = dot(rows_v[...], wg[j, :, cols])
        b = dot(rows_v[...], wu[j, :, cols])
        act_a[:, act_of(u)] = (a * jax.nn.sigmoid(a) * b).astype(BF16)
        return carry

    lax.fori_loop(0, 4, hidden_f, 0)

    def column_f(n):
        cols = pl.ds(pl.multiple_of(n * BLOCK, BLOCK), BLOCK)
        total = jnp.zeros((ROWS, BLOCK), F32)
        for j in range(2):
            total += dot(act_a[:, j * UNIT : (j + 1) * UNIT], wd[j, :, cols])
        return total

    emit_all(column_f, ret_f, got_f, tf_send, tf_recv)

    def hop(c, h, wide, src, dst, section, send_sem, recv_sem):
        cols = pl.ds(h * HALF + 2 * BLOCK * c, wide)
        return pltpu.make_async_remote_copy(
            src_ref=src.at[:, cols],
            dst_ref=dst.at[:, cols],
            send_sem=send_sem.at[2 * c + h],
            recv_sem=recv_sem.at[2 * c + h],
            device_id=(section, me),
            device_id_type=MESH,
        )

    def hops(src, dst, section, send_sem, recv_sem):
        return [
            hop(c, h, 2 * BLOCK if c < CHUNKS - 1 else BLOCK, src, dst, section, send_sem, recv_sem)
            for c in range(CHUNKS)
            for h in range(2)
        ]

    def combine(got, recv_sem, kinds, base, total, moves):
        for c in range(CHUNKS):
            wide = 2 * BLOCK if c < CHUNKS - 1 else BLOCK
            here = got.at[c, :, :, pl.ds(0, wide + LANES)]
            pltpu.make_async_copy(here, here, recv_sem.at[c]).wait()
            pieces = wide // LANES
            rows = got[c, :, :, :wide].reshape(MSG, wide)
            tail = got[c, :, :, wide : wide + LANES].reshape(MSG, LANES)
            main = sum(dot(hot_m[i], rows) for i in kinds)
            rest = sum(dot(hot_r[i, : 2 * pieces * TOK], tail) for i in kinds)
            for h in range(2):
                for i in range(pieces):
                    at = h * HALF + 2 * BLOCK * c + i * LANES
                    k = h * pieces + i
                    total[:, at : at + LANES] = (
                        base[:, at : at + LANES].astype(F32)
                        + main[h * TOK : (h + 1) * TOK, i * LANES : (i + 1) * LANES]
                        + rest[k * TOK : (k + 1) * TOK]
                    ).astype(BF16)
                moves[2 * c + h].start()

    moves_b = hops(sum_b, out_b, below, hb_send, hb_recv)
    moves_f = hops(sum_f, out_f, above, hf_send, hf_recv)
    for copy in bases:
        copy.wait()
    combine(got_b, tb_recv, (0,), base_c, sum_b, moves_b)
    combine(got_f, tf_recv, (1, 2), base_x, sum_f, moves_f)

    for k in FAR_FIRST:
        expert_v(k).wait_send()
        expert_f(k).wait_send()
    for copy in exchange:
        copy.wait_send()
    for ret, send_sem in ((ret_b, tb_send), (ret_f, tf_send)):
        for c in range(CHUNKS):
            wide = 2 * BLOCK if c < CHUNKS - 1 else BLOCK
            sent = ret.at[c, pl.ds(0, CHIPS - 1), :, pl.ds(0, wide + LANES)]
            pltpu.make_async_copy(sent, sent, send_sem.at[c]).wait()
    for copy in moves_b + moves_f:
        copy.wait()


def write_out(f, b, out_f, out_b, held, in_sem, out_sem):
    half = TOK // 2
    parts = [(i, pl.ds(j * half, half)) for i in range(2) for j in range(2)]
    loads = [
        pltpu.make_async_copy((f, b)[i].at[rows], held.at[i, rows], in_sem.at[n])
        for n, (i, rows) in enumerate(parts)
    ]
    stores = [
        pltpu.make_async_copy(held.at[i, rows], (out_f, out_b)[i].at[0, rows], out_sem.at[n])
        for n, (i, rows) in enumerate(parts)
    ]
    for load in loads:
        load.start()
    for load, store in zip(loads, stores):
        load.wait()
        store.start()
    for store in stores:
        store.wait()


def body(
    fwd_input, fwd_experts, fwd_gates, bwd_input, bwd_cotangent, bwd_experts, bwd_gates,
    w_gate, w_up, w_down,
):
    vmem, anywhere = pl.BlockSpec(memory_space=pltpu.VMEM), pl.BlockSpec(memory_space=pl.ANY)
    token_rows = jax.ShapeDtypeStruct((TOK, D), BF16)
    rows = pltpu.VMEM((TOK, D), BF16)
    messages = pltpu.VMEM((CHIPS, 16, WIDE), BF16)
    chunks = pltpu.VMEM((CHUNKS, CHIPS, 16, CHUNK), BF16)
    dma = pltpu.SemaphoreType.DMA
    out_f, out_b = pl.pallas_call(
        kernel,
        out_shape=(token_rows, token_rows),
        in_specs=[vmem] * 4 + [anywhere] * 6,
        out_specs=(anywhere, anywhere),
        scratch_shapes=[
            pltpu.VMEM((3, 2 * TOK, HALF), BF16),
            pltpu.VMEM((3, PIECES * TOK, PIECE), BF16),
        ]
        + [messages] * 6
        + [chunks] * 4
        + [
            pltpu.VMEM((2, D, UNIT), BF16),
            pltpu.VMEM((2, D, UNIT), BF16),
            pltpu.VMEM((2, UNIT, D), BF16),
            pltpu.VMEM((ROWS, D), BF16),
            pltpu.VMEM((ROWS, D), BF16),
            pltpu.VMEM((ROWS, 2 * UNIT), BF16),
            pltpu.VMEM((ROWS, 2 * UNIT), BF16),
            rows, rows, rows, rows,
            pltpu.VMEM((3, 2 * TOK, MSG), BF16),
            pltpu.VMEM((3, 8 * TOK, MSG), BF16),
            dma((27,)), dma((2,)), dma((3,)), dma((3,)), dma((3,)), dma((3,)),
        ]
        + [dma((CHIPS,))] * 6
        + [dma((CHUNKS,))] * 4
        + [dma((2 * CHUNKS,))] * 4,
        compiler_params=pltpu.CompilerParams(
            collective_id=0, has_side_effects=True, vmem_limit_bytes=60 << 20
        ),
        name="relay_experts",
    )(
        fwd_experts[0].T, fwd_gates[0].T, bwd_experts[0].T, bwd_gates[0].T,
        fwd_input[0], bwd_input[0], bwd_cotangent[0], w_gate[0], w_up[0], w_down[0],
    )
    result = jax.ShapeDtypeStruct((1, TOK, D), BF16)
    return pl.pallas_call(
        write_out,
        out_shape=(result, result),
        in_specs=[anywhere] * 2,
        out_specs=(anywhere, anywhere),
        scratch_shapes=[pltpu.VMEM((2, TOK, D), BF16), dma((4,)), dma((4,))],
        compiler_params=pltpu.CompilerParams(vmem_limit_bytes=60 << 20),
        name="write_out",
    )(out_f, out_b)


def solution(mesh):
    tokens = P("pp", "ep", None)
    in_specs = (tokens,) * 7 + (P("pp", None, "ep"), P("pp", None, "ep"), tokens)
    return jax.shard_map(
        body, mesh=mesh, in_specs=in_specs, out_specs=(tokens, tokens), check_vma=False
    )
```

```python
import jax
import jax.numpy as jnp
from jax import lax
from jax.experimental import pallas as pl
from jax.experimental.pallas import tpu as pltpu
from jax.sharding import PartitionSpec as P

MESH = pl.DeviceIdType.MESH
F32 = jnp.float32
BF16 = jnp.bfloat16

D = 3584
UNIT = 512
TOK = 64
CHIPS = 16
SIDE = 4
ROWS = 160
HALF = D // 2
PIECE = 512
PIECES = D // PIECE
WIDE = HALF + PIECE
MSG = CHIPS * 16
BLOCK = 256
LANES = 128
CHUNKS = 4
CHUNK = 2 * BLOCK + LANES
JOINT = 4
JOINT_PIECE = D // JOINT
GROUPS_F = 2 + 8
GROUPS_B = GROUPS_F + 2 * JOINT
FAR_FIRST = (10, 9, 14, 11, 6, 5, 13, 15, 7, 8, 2, 4, 1, 12, 3)


def dot(a, b):
    return lax.dot_general(a, b, (((1,), (0,)), ((), ())), preferred_element_type=F32)


def dot_nt(a, b):
    return lax.dot_general(a, b, (((1,), (1,)), ((), ())), preferred_element_type=F32)


def iota(shape, dim):
    return lax.broadcasted_iota(jnp.int32, shape, dim)


def as_hot(mask):
    return jnp.where(mask, 1.0, 0.0).astype(BF16)


def routing(ids, groups):
    expert = iota((CHIPS, TOK), 0)
    first, second = ids[0:1, :] == expert, ids[1:2, :] == expert
    hits = jnp.where(first | second, 1.0, 0.0)
    before = as_hot(iota((TOK, TOK), 0) < iota((TOK, TOK), 1))
    keys = hits * (dot(hits.astype(BF16), before) + 1.0)
    hots = groups * TOK
    copies = as_hot((iota((TOK, hots), 1) & (TOK - 1)) == iota((TOK, hots), 0))
    wide = dot(keys.astype(BF16), copies).astype(BF16)
    key = dot(rows_of_expert(BF16), wide)
    slot = iota((MSG, hots), 0) & 15
    group = iota((MSG, hots), 1) >> 6
    first_slot = (group - 2) * 2
    if groups > GROUPS_F:
        joint = group - GROUPS_F
        joint = jnp.where(joint < JOINT, joint * 4, (joint - JOINT) * 4 + 2)
        first_slot = jnp.where(group < GROUPS_F, first_slot, joint)
    want_main = (slot - 8 * group).astype(F32)
    want_rest = (slot - first_slot).astype(F32)
    main = (want_main >= 0.0) & (want_main < 8.0) & (key == want_main + 1.0)
    rest = (want_rest >= 0.0) & (want_rest < 2.0) & (key == want_rest + 9.0)
    hot = as_hot(main | rest)
    return key[:, :TOK], hot, first, second


def rows_of_expert(dtype):
    row, expert = iota((MSG, CHIPS), 0), iota((MSG, CHIPS), 1)
    return jnp.where((row >> 4) == expert, 1.0, 0.0).astype(dtype)


def slot_gates(key, first, second, gates):
    per = jnp.where(first, gates[0:1, :], 0.0) + jnp.where(second, gates[1:2, :], 0.0)
    spread = lax.dot_general(
        rows_of_expert(F32),
        per,
        (((1,), (0,)), ((), ())),
        precision=lax.Precision.HIGHEST,
        preferred_element_type=F32,
    )
    slot = iota((MSG, TOK), 0)
    main = key == (slot & 7).astype(F32) + 1.0
    rest = key == (slot & 1).astype(F32) + 9.0
    return (
        jnp.sum(jnp.where(main, spread, 0.0), axis=1, keepdims=True),
        jnp.sum(jnp.where(rest, spread, 0.0), axis=1, keepdims=True),
    )


def place(u, v):
    return (((u >> 1) & 15) << 4) + ((u >> 5) << 1) + (u & 1) == v


def place_joint(u, v):
    return (((u >> 1) & 15) << 4) + ((u >> 6) << 2) + (((u >> 5) & 1) << 1) + (u & 1) == v


def kernel(
    fids_in, fgates_in, bids_in, bgates_in, xf, xb, cb, gate, up, down,
    out_f, out_b,
    fids, fgates, bids, bgates, half_x, piece_x, joint_x, send_v, send_s, send_f, recv_v, recv_s, recv_f, ret_b, ret_f, got_b, got_f,
    wg, wu, wd, rows_f, rows_v, rows_s, pre_a, pre_b, act_a, act_b,
    base_x, base_c, sum_f, sum_b, hot_m, hot_r,
    small_sem, in_sem, joint_sem, base_sem, w_sem, own_sem, wx_send, wx_recv,
    sv_sem, rv_sem, ss_sem, rs_sem, sf_sem, rf_sem,
    tb_send, tb_recv, tf_send, tf_recv, hb_send, hb_recv, hf_send, hf_recv, ready,
):
    z, me = lax.axis_index("pp"), lax.axis_index("ep")
    sections = lax.axis_size("pp")
    chip, core = me // 2, lax.rem(me, 2)
    above, below = lax.rem(z + 1, sections), lax.rem(z + sections - 1, sections)
    sibling = chip * 2 + 1 - core

    def peer(k):
        x = lax.rem(chip // SIDE + k // SIDE, SIDE)
        y = lax.rem(lax.rem(chip, SIDE) + k % SIDE, SIDE)
        return x * SIDE + y

    barrier = pltpu.get_barrier_semaphore()
    for k in FAR_FIRST:
        pl.semaphore_signal(
            barrier, inc=1, device_id=(z, peer(k) * 2 + core), device_id_type=MESH
        )
    for target in ((z, sibling), (below, me)):
        pl.semaphore_signal(barrier, inc=1, device_id=target, device_id_type=MESH)

    small = [
        pltpu.make_async_copy(src, dst, small_sem.at[i])
        for i, (src, dst) in enumerate(
            ((fids_in, fids), (fgates_in, fgates), (bids_in, bids), (bgates_in, bgates))
        )
    ]
    loads = []
    for i, src in enumerate((xf, xb, cb)):
        own = [
            pltpu.make_async_copy(
                src.at[:, pl.ds(h * HALF, HALF)],
                half_x.at[i, pl.ds(h * TOK, TOK)],
                in_sem.at[i * 2 + h],
            )
            for h in range(2)
        ]
        pieces, width, at = (
            (piece_x, PIECE, 2 * JOINT)
            if i == 0
            else (joint_x.at[i - 1], JOINT_PIECE, (i - 1) * JOINT)
        )
        for k in range(D // width):
            own.append(
                pltpu.make_async_copy(
                    src.at[:, pl.ds(k * width, width)],
                    pieces.at[pl.ds(k * TOK, TOK)],
                    joint_sem.at[at + k],
                )
            )
        loads.append(own)
    for copy in small[:1] + loads[0] + small[1:] + loads[1] + loads[2]:
        copy.start()

    weights = [
        pltpu.make_async_copy(src, dst.at[0], w_sem.at[i])
        for i, (src, dst) in enumerate(((gate, wg), (up, wu), (down, wd)))
    ]
    bases = [
        pltpu.make_async_copy(xf, base_x, base_sem.at[0]),
        pltpu.make_async_copy(cb, base_c, base_sem.at[1]),
    ]

    def fill(dst, at, rows):
        width = rows.shape[1]
        dst[:, :, at : at + width] = rows.astype(BF16).reshape(CHIPS, 16, width)

    def to_expert(k, src, dst, send_sem, recv_sem):
        q = peer(k)
        return pltpu.make_async_remote_copy(
            src_ref=src.at[q],
            dst_ref=dst.at[chip],
            send_sem=send_sem.at[k],
            recv_sem=recv_sem.at[k],
            device_id=(z, q * 2 + core),
            device_id_type=MESH,
        )

    def expert_v(k):
        return to_expert(k, send_v, recv_v, sv_sem, rv_sem)

    def expert_s(k):
        return to_expert(k, send_s, recv_s, ss_sem, rs_sem)

    def expert_f(k):
        return to_expert(k, send_f, recv_f, sf_sem, rf_sem)

    keep_v, keep_s, keep_f = (
        pltpu.make_async_copy(src.at[chip], dst.at[chip], own_sem.at[i])
        for i, (src, dst) in enumerate(((send_v, recv_v), (send_s, recv_s), (send_f, recv_f)))
    )

    small[0].wait()
    key_f, hot_f, first_f, second_f = routing(fids[...], GROUPS_F)
    for copy in loads[0]:
        copy.wait()
    fill(send_f, 0, dot(hot_f[:, : 2 * TOK], half_x[0]))
    fill(send_f, HALF, dot(hot_f[:, 2 * TOK : 2 * TOK + PIECES * TOK], piece_x[...]))
    pl.semaphore_wait(barrier, CHIPS - 1 + 2)
    for k in FAR_FIRST:
        expert_f(k).start()
    keep_f.start()

    exchange = [
        pltpu.make_async_remote_copy(
            src_ref=src,
            dst_ref=dst.at[1],
            send_sem=wx_send.at[i],
            recv_sem=wx_recv.at[i],
            device_id=(z, sibling),
            device_id_type=MESH,
        )
        for i, (src, dst) in enumerate(((gate, wg), (up, wu), (down, wd)))
    ]
    for copy in weights + exchange + bases:
        copy.start()

    pl.semaphore_signal(ready, inc=1, device_id=(above, me), device_id_type=MESH)
    for copy in small[1:] + loads[1] + loads[2]:
        copy.wait()
    key_b, hot_b, first_b, second_b = routing(bids[...], GROUPS_B)
    scale_m, scale_r = slot_gates(key_b, first_b, second_b, bgates[...])
    joint_v = hot_b[:, GROUPS_F * TOK : (GROUPS_F + JOINT) * TOK]
    joint_s = hot_b[:, (GROUPS_F + JOINT) * TOK :]
    fill(send_v, 0, dot(hot_b[:, : 2 * TOK], half_x[1]))
    fill(send_v, HALF, dot(joint_v, joint_x[0]) + dot(joint_s, joint_x[1]) * scale_r)
    for k in FAR_FIRST:
        expert_f(k).wait_send()
        expert_v(k).start()
    keep_v.start()
    fill(send_s, 0, dot(hot_b[:, : 2 * TOK], half_x[2]) * scale_m)

    def flip(hot):
        n = hot.shape[1]
        unit = as_hot(iota((n, n), 0) == iota((n, n), 1))
        return dot_nt(unit, hot).astype(BF16)

    hot_m[0] = flip(hot_b[:, : 2 * TOK])
    hot_r[0] = flip(hot_b[:, 2 * TOK : GROUPS_F * TOK])
    scale_m, scale_r = slot_gates(key_f, first_f, second_f, fgates[...])
    high_m, high_r = scale_m.astype(BF16).astype(F32), scale_r.astype(BF16).astype(F32)
    hot_main, hot_rest = hot_f[:, : 2 * TOK].astype(F32), hot_f[:, 2 * TOK :].astype(F32)
    hot_m[1] = flip((hot_main * high_m).astype(BF16))
    hot_r[1] = flip((hot_rest * high_r).astype(BF16))
    hot_m[2] = flip((hot_main * (scale_m - high_m)).astype(BF16))
    hot_r[2] = flip((hot_rest * (scale_r - high_r)).astype(BF16))
    for k in FAR_FIRST:
        expert_v(k).wait_send()
        expert_s(k).start()
    keep_s.start()

    def unpack(src, dst):
        def step(i, carry):
            pair = src[pl.ds(2 * i, 2), :, :HALF].astype(F32)
            halves = pair.reshape(2, 2, 8, HALF)
            rows = pl.ds(pl.multiple_of(16 * i, 16), 16)
            dst[rows, :HALF] = halves[:, 0].reshape(16, HALF).astype(BF16)
            dst[rows, HALF:] = halves[:, 1].reshape(16, HALF).astype(BF16)
            return carry

        lax.fori_loop(0, CHIPS // 2, step, 0)

    def unit_of(u):
        return u // 2, pl.ds(pl.multiple_of(lax.rem(u, 2) * BLOCK, BLOCK), BLOCK)

    def act_of(u):
        return pl.ds(pl.multiple_of(u * BLOCK, BLOCK), BLOCK)

    def to_token(k, c, width, src, dst, send_sem, recv_sem):
        q = peer(k)
        return pltpu.make_async_remote_copy(
            src_ref=src.at[c, q, :, pl.ds(0, width)],
            dst_ref=dst.at[c, chip, :, pl.ds(0, width)],
            send_sem=send_sem.at[c],
            recv_sem=recv_sem.at[c],
            device_id=(z, q * 2 + core),
            device_id_type=MESH,
        )

    def emit(column, c, steps, ret):
        lows = [column(2 * c + i) for i in range(steps)]
        highs = [column(2 * c + i + 7) for i in range(steps)]
        for i in range(steps):
            main = jnp.concatenate(
                [y[:128].reshape(CHIPS, 8, BLOCK) for y in (lows[i], highs[i])], axis=1
            )
            ret[c, :, :, i * BLOCK : (i + 1) * BLOCK] = main.astype(BF16)
        rests = [
            y[128:, j * LANES : (j + 1) * LANES] for y in lows + highs for j in range(BLOCK // LANES)
        ]
        n = len(rests) * 32
        order = as_hot(place(iota((MSG, n), 1), iota((MSG, n), 0)))
        rest = dot(order, jnp.concatenate(rests, axis=0).astype(BF16))
        wide = steps * BLOCK
        ret[c, :, :, wide : wide + LANES] = rest.astype(BF16).reshape(CHIPS, 16, LANES)

    def keep(c, wide, ret, got, recv_sem):
        return pltpu.make_async_copy(
            ret.at[c, chip, :, pl.ds(0, wide + LANES)],
            got.at[c, chip, :, pl.ds(0, wide + LANES)],
            recv_sem.at[c],
        )

    widths = (2 * BLOCK,) * (CHUNKS - 1) + (BLOCK,)

    def hidden_ab(u, carry):
        j, cols = unit_of(u)
        pre_a[u] = dot(rows_v[...], wg[j, :, cols])
        pre_b[u] = dot(rows_v[...], wu[j, :, cols])
        return carry

    def hidden_f(u, carry):
        j, cols = unit_of(u)
        a = dot(rows_f[...], wg[j, :, cols])
        b = dot(rows_f[...], wu[j, :, cols])
        act_a[:, act_of(u)] = (a * jax.nn.sigmoid(a) * b).astype(BF16)
        return carry

    def hidden_b(u, carry):
        j, cols = unit_of(u)
        a, b = pre_a[u], pre_b[u]
        dh = dot_nt(rows_s[...], wd[j, cols, :])
        sig = jax.nn.sigmoid(a)
        act_a[:, act_of(u)] = (dh * b * sig * (1.0 + a * (1.0 - sig))).astype(BF16)
        act_b[:, act_of(u)] = (dh * (a * sig)).astype(BF16)
        return carry

    def column_f(n):
        cols = pl.ds(pl.multiple_of(n * BLOCK, BLOCK), BLOCK)
        total = jnp.zeros((ROWS, BLOCK), F32)
        for j in range(2):
            total += dot(act_a[:, j * UNIT : (j + 1) * UNIT], wd[j, :, cols])
        return total

    def column_b(n):
        rows = pl.ds(pl.multiple_of(n * BLOCK, BLOCK), BLOCK)
        total = jnp.zeros((ROWS, BLOCK), F32)
        for j in range(2):
            total += dot_nt(act_a[:, j * UNIT : (j + 1) * UNIT], wg[j, rows, :])
            total += dot_nt(act_b[:, j * UNIT : (j + 1) * UNIT], wu[j, rows, :])
        return total

    for k in FAR_FIRST:
        expert_f(k).wait_recv()
    keep_f.wait()
    unpack(recv_f, rows_f)
    n = PIECES * 32
    order = as_hot(place(iota((n, MSG), 0), iota((n, MSG), 1)))
    plain = dot(order, recv_f[:, :, HALF:].reshape(MSG, PIECE)).astype(BF16)
    for k in range(PIECES):
        rows_f[128:ROWS, k * PIECE : (k + 1) * PIECE] = plain[32 * k : 32 * k + 32]
    for copy in weights:
        copy.wait()
    lax.fori_loop(0, 2, hidden_f, 0)
    for copy in exchange:
        copy.wait_recv()
    lax.fori_loop(2, 4, hidden_f, 0)

    def step_f(c, carry):
        emit(column_f, c, 2, ret_f)
        return carry

    lax.fori_loop(0, CHUNKS - 1, step_f, 0)
    emit(column_f, CHUNKS - 1, 1, ret_f)

    for k in FAR_FIRST:
        expert_v(k).wait_recv()
    keep_v.wait()
    unpack(recv_v, rows_v)
    order = as_hot(place_joint(iota((MSG, MSG), 0), iota((MSG, MSG), 1)))
    plain = dot(order, recv_v[:, :, HALF:].reshape(MSG, JOINT_PIECE)).astype(BF16)
    for k in range(JOINT):
        cols = slice(k * JOINT_PIECE, (k + 1) * JOINT_PIECE)
        rows_v[128:ROWS, cols] = plain[64 * k : 64 * k + 32]
        rows_s[128:ROWS, cols] = plain[64 * k + 32 : 64 * k + 64]
    lax.fori_loop(0, 4, hidden_ab, 0)
    for k in FAR_FIRST:
        expert_s(k).wait_send()
        for c, wide in enumerate(widths):
            to_token(k, c, wide + LANES, ret_f, got_f, tf_send, tf_recv).start()
    for c, wide in enumerate(widths):
        keep(c, wide, ret_f, got_f, tf_recv).start()
    for k in FAR_FIRST:
        expert_s(k).wait_recv()
    keep_s.wait()
    unpack(recv_s, rows_s)
    lax.fori_loop(0, 4, hidden_b, 0)

    def send_back(c, wide):
        for k in FAR_FIRST:
            to_token(k, c, wide + LANES, ret_b, got_b, tb_send, tb_recv).start()
        keep(c, wide, ret_b, got_b, tb_recv).start()

    def step_b(c, carry):
        emit(column_b, c, 2, ret_b)
        send_back(c, 2 * BLOCK)
        return carry

    lax.fori_loop(0, CHUNKS - 1, step_b, 0)
    emit(column_b, CHUNKS - 1, 1, ret_b)
    send_back(CHUNKS - 1, BLOCK)

    def hop(c, h, wide, src, dst, section, send_sem, recv_sem):
        cols = pl.ds(h * HALF + 2 * BLOCK * c, wide)
        return pltpu.make_async_remote_copy(
            src_ref=src.at[:, cols],
            dst_ref=dst.at[:, cols],
            send_sem=send_sem.at[2 * c + h],
            recv_sem=recv_sem.at[2 * c + h],
            device_id=(section, me),
            device_id_type=MESH,
        )

    def hops(src, dst, section, send_sem, recv_sem):
        return [
            hop(c, h, 2 * BLOCK if c < CHUNKS - 1 else BLOCK, src, dst, section, send_sem, recv_sem)
            for c in range(CHUNKS)
            for h in range(2)
        ]

    def combine(got, recv_sem, kinds, base, total, moves):
        for c in range(CHUNKS):
            wide = 2 * BLOCK if c < CHUNKS - 1 else BLOCK
            here = got.at[c, :, :, pl.ds(0, wide + LANES)]
            pltpu.make_async_copy(here, here, recv_sem.at[c]).wait()
            pieces = wide // LANES
            rows = got[c, :, :, :wide].reshape(MSG, wide)
            tail = got[c, :, :, wide : wide + LANES].reshape(MSG, LANES)
            main = sum(dot(hot_m[i], rows) for i in kinds)
            rest = sum(dot(hot_r[i, : 2 * pieces * TOK], tail) for i in kinds)
            for h in range(2):
                for i in range(pieces):
                    at = h * HALF + 2 * BLOCK * c + i * LANES
                    k = h * pieces + i
                    total[:, at : at + LANES] = (
                        base[:, at : at + LANES].astype(F32)
                        + main[h * TOK : (h + 1) * TOK, i * LANES : (i + 1) * LANES]
                        + rest[k * TOK : (k + 1) * TOK]
                    ).astype(BF16)
                moves[2 * c + h].start()

    moves_b = hops(sum_b, out_b, below, hb_send, hb_recv)
    moves_f = hops(sum_f, out_f, above, hf_send, hf_recv)
    for copy in bases:
        copy.wait()
    combine(got_f, tf_recv, (1, 2), base_x, sum_f, moves_f)
    pl.semaphore_wait(ready, 1)
    combine(got_b, tb_recv, (0,), base_c, sum_b, moves_b)

    for copy in exchange:
        copy.wait_send()
    for ret, send_sem in ((ret_b, tb_send), (ret_f, tf_send)):
        for c in range(CHUNKS):
            wide = 2 * BLOCK if c < CHUNKS - 1 else BLOCK
            sent = ret.at[c, pl.ds(0, CHIPS - 1), :, pl.ds(0, wide + LANES)]
            pltpu.make_async_copy(sent, sent, send_sem.at[c]).wait()
    for copy in moves_b + moves_f:
        copy.wait()


def body(
    fwd_input, fwd_experts, fwd_gates, bwd_input, bwd_cotangent, bwd_experts, bwd_gates,
    w_gate, w_up, w_down,
):
    vmem, anywhere = pl.BlockSpec(memory_space=pltpu.VMEM), pl.BlockSpec(memory_space=pl.ANY)
    rows = pltpu.VMEM((TOK, D), BF16)
    messages = pltpu.VMEM((CHIPS, 16, WIDE), BF16)
    joint = pltpu.VMEM((CHIPS, 16, HALF + JOINT_PIECE), BF16)
    halves = pltpu.VMEM((CHIPS, 16, HALF), BF16)
    chunks = pltpu.VMEM((CHUNKS, CHIPS, 16, CHUNK), BF16)
    dma = pltpu.SemaphoreType.DMA
    out_f, out_b = pl.pallas_call(
        kernel,
        out_shape=(rows, rows),
        in_specs=[anywhere] * 10,
        out_specs=(vmem, vmem),
        scratch_shapes=[
            pltpu.VMEM((2, TOK), jnp.int32),
            pltpu.VMEM((2, TOK), F32),
            pltpu.VMEM((2, TOK), jnp.int32),
            pltpu.VMEM((2, TOK), F32),
            pltpu.VMEM((3, 2 * TOK, HALF), BF16),
            pltpu.VMEM((PIECES * TOK, PIECE), BF16),
            pltpu.VMEM((2, JOINT * TOK, JOINT_PIECE), BF16),
        ]
        + [joint, halves, messages] * 2
        + [chunks] * 4
        + [
            pltpu.VMEM((2, D, UNIT), BF16),
            pltpu.VMEM((2, D, UNIT), BF16),
            pltpu.VMEM((2, UNIT, D), BF16),
            pltpu.VMEM((ROWS, D), BF16),
            pltpu.VMEM((ROWS, D), BF16),
            pltpu.VMEM((ROWS, D), BF16),
            pltpu.VMEM((4, ROWS, BLOCK), F32),
            pltpu.VMEM((4, ROWS, BLOCK), F32),
            pltpu.VMEM((ROWS, 2 * UNIT), BF16),
            pltpu.VMEM((ROWS, 2 * UNIT), BF16),
            rows, rows, rows, rows,
            pltpu.VMEM((3, 2 * TOK, MSG), BF16),
            pltpu.VMEM((3, 8 * TOK, MSG), BF16),
            dma((4,)), dma((6,)), dma((2 * JOINT + PIECES,)), dma((2,)), dma((3,)), dma((3,)), dma((3,)), dma((3,)),
        ]
        + [dma((CHIPS,))] * 6
        + [dma((CHUNKS,))] * 4
        + [dma((2 * CHUNKS,))] * 4
        + [pltpu.SemaphoreType.REGULAR],
        compiler_params=pltpu.CompilerParams(
            collective_id=0, has_side_effects=True, vmem_limit_bytes=60 << 20
        ),
        name="relay_experts",
    )(
        fwd_experts[0].T, fwd_gates[0].T, bwd_experts[0].T, bwd_gates[0].T,
        fwd_input[0], bwd_input[0], bwd_cotangent[0], w_gate[0], w_up[0], w_down[0],
    )
    return out_f[None], out_b[None]


def solution(mesh):
    tokens = P("pp", "ep", None)
    in_specs = (tokens,) * 7 + (P("pp", None, "ep"), P("pp", None, "ep"), tokens)
    return jax.shard_map(
        body, mesh=mesh, in_specs=in_specs, out_specs=(tokens, tokens), check_vma=False
    )
```

```python
import jax
import jax.numpy as jnp
from jax import lax
from jax.experimental import pallas as pl
from jax.experimental.pallas import tpu as pltpu
from jax.sharding import PartitionSpec as P

MESH = pl.DeviceIdType.MESH
F32 = jnp.float32
BF16 = jnp.bfloat16

D = 3584
UNIT = 512
TOK = 64
CHIPS = 16
SIDE = 4
ROWS = 160
HALF = D // 2
PIECE = 512
PIECES = D // PIECE
WIDE = HALF + PIECE
MSG = CHIPS * 16
BLOCK = 256
LANES = 128
CHUNKS = 4
EARLY = 2
CHUNK = 2 * BLOCK + LANES
JOINT = 4
JOINT_PIECE = D // JOINT
GROUPS_F = 2 + 8
GROUPS_B = GROUPS_F + 2 * JOINT
FAR_FIRST = (10, 9, 14, 11, 6, 5, 13, 15, 7, 8, 2, 4, 1, 12, 3)


def dot(a, b):
    return lax.dot_general(a, b, (((1,), (0,)), ((), ())), preferred_element_type=F32)


def dot_nt(a, b):
    return lax.dot_general(a, b, (((1,), (1,)), ((), ())), preferred_element_type=F32)


def iota(shape, dim):
    return lax.broadcasted_iota(jnp.int32, shape, dim)


def as_hot(mask):
    return jnp.where(mask, 1.0, 0.0).astype(BF16)


def routing(ids, groups):
    expert = iota((CHIPS, TOK), 0)
    first, second = ids[0:1, :] == expert, ids[1:2, :] == expert
    hits = jnp.where(first | second, 1.0, 0.0)
    before = as_hot(iota((TOK, TOK), 0) < iota((TOK, TOK), 1))
    keys = hits * (dot(hits.astype(BF16), before) + 1.0)
    hots = groups * TOK
    copies = as_hot((iota((TOK, hots), 1) & (TOK - 1)) == iota((TOK, hots), 0))
    wide = dot(keys.astype(BF16), copies).astype(BF16)
    key = dot(rows_of_expert(BF16), wide)
    slot = iota((MSG, hots), 0) & 15
    group = iota((MSG, hots), 1) >> 6
    first_slot = (group - 2) * 2
    if groups > GROUPS_F:
        joint = group - GROUPS_F
        joint = jnp.where(joint < JOINT, joint * 4, (joint - JOINT) * 4 + 2)
        first_slot = jnp.where(group < GROUPS_F, first_slot, joint)
    want_main = (slot - 8 * group).astype(F32)
    want_rest = (slot - first_slot).astype(F32)
    main = (want_main >= 0.0) & (want_main < 8.0) & (key == want_main + 1.0)
    rest = (want_rest >= 0.0) & (want_rest < 2.0) & (key == want_rest + 9.0)
    hot = as_hot(main | rest)
    return key[:, :TOK], hot, first, second


def rows_of_expert(dtype):
    row, expert = iota((MSG, CHIPS), 0), iota((MSG, CHIPS), 1)
    return jnp.where((row >> 4) == expert, 1.0, 0.0).astype(dtype)


def slot_gates(key, first, second, gates):
    per = jnp.where(first, gates[0:1, :], 0.0) + jnp.where(second, gates[1:2, :], 0.0)
    spread = lax.dot_general(
        rows_of_expert(F32),
        per,
        (((1,), (0,)), ((), ())),
        precision=lax.Precision.HIGHEST,
        preferred_element_type=F32,
    )
    slot = iota((MSG, TOK), 0)
    main = key == (slot & 7).astype(F32) + 1.0
    rest = key == (slot & 1).astype(F32) + 9.0
    return (
        jnp.sum(jnp.where(main, spread, 0.0), axis=1, keepdims=True),
        jnp.sum(jnp.where(rest, spread, 0.0), axis=1, keepdims=True),
    )


def place(u, v):
    return (((u >> 1) & 15) << 4) + ((u >> 5) << 1) + (u & 1) == v


def place_joint(u, v):
    return (((u >> 1) & 15) << 4) + ((u >> 6) << 2) + (((u >> 5) & 1) << 1) + (u & 1) == v


def kernel(
    fids_in, fgates_in, bids_in, bgates_in, xf, xb, cb, gate, up, down,
    out,
    fids, fgates, bids, bgates, half_x, piece_x, joint_x, send_v, send_s, send_f, recv_v, recv_s, recv_f, ret_b, ret_f, got_b, got_f,
    wg, wu, wd, rows_f, rows_v, rows_s, pre_a, pre_b, act_a, act_b,
    base_x, base_c, sum_f, sum_b, hot_m, hot_r,
    small_sem, in_sem, joint_sem, base_sem, w_sem, own_sem, wx_send, wx_recv,
    sv_sem, rv_sem, ss_sem, rs_sem, sf_sem, rf_sem,
    tb_send, tb_recv, tf_send, tf_recv, hb_send, hb_recv, hf_send, hf_recv, ready,
):
    z, me = lax.axis_index("pp"), lax.axis_index("ep")
    sections = lax.axis_size("pp")
    chip, core = me // 2, lax.rem(me, 2)
    above, below = lax.rem(z + 1, sections), lax.rem(z + sections - 1, sections)
    last = sections - 1
    upward = z <= sections // 2
    sibling = chip * 2 + 1 - core

    def peer(k):
        x = lax.rem(chip // SIDE + k // SIDE, SIDE)
        y = lax.rem(lax.rem(chip, SIDE) + k % SIDE, SIDE)
        return x * SIDE + y

    small = [
        pltpu.make_async_copy(src, dst, small_sem.at[i])
        for i, (src, dst) in enumerate(
            ((fids_in, fids), (fgates_in, fgates), (bids_in, bids), (bgates_in, bgates))
        )
    ]
    loads = []
    for i, src in enumerate((xf, xb, cb)):
        own = [
            pltpu.make_async_copy(
                src.at[:, pl.ds(h * HALF, HALF)],
                half_x.at[i, pl.ds(h * TOK, TOK)],
                in_sem.at[i * 2 + h],
            )
            for h in range(2)
        ]
        pieces, width, at = (
            (piece_x, PIECE, 2 * JOINT)
            if i == 0
            else (joint_x.at[i - 1], JOINT_PIECE, (i - 1) * JOINT)
        )
        for k in range(D // width):
            own.append(
                pltpu.make_async_copy(
                    src.at[:, pl.ds(k * width, width)],
                    pieces.at[pl.ds(k * TOK, TOK)],
                    joint_sem.at[at + k],
                )
            )
        loads.append(own)
    for copy in small[:1] + loads[0]:
        copy.start()
    barrier = pltpu.get_barrier_semaphore()
    for k in FAR_FIRST:
        pl.semaphore_signal(
            barrier, inc=1, device_id=(z, peer(k) * 2 + core), device_id_type=MESH
        )
    pl.semaphore_signal(barrier, inc=1, device_id=(z, sibling), device_id_type=MESH)

    @pl.when(z < last)
    def _():
        pl.semaphore_signal(barrier, inc=1, device_id=(above, me), device_id_type=MESH)

    @pl.when(z == 0)
    def _():
        pl.semaphore_signal(barrier, inc=1, device_id=(below, me), device_id_type=MESH)


    for copy in small[1:] + loads[1] + loads[2]:
        copy.start()

    weights = [
        pltpu.make_async_copy(src, dst.at[0], w_sem.at[i])
        for i, (src, dst) in enumerate(((gate, wg), (up, wu), (down, wd)))
    ]
    bases = [
        pltpu.make_async_copy(xf, base_x, base_sem.at[0]),
        pltpu.make_async_copy(cb, base_c, base_sem.at[1]),
    ]

    def fill(dst, at, rows):
        width = rows.shape[1]
        dst[:, :, at : at + width] = rows.astype(BF16).reshape(CHIPS, 16, width)

    def to_expert(k, src, dst, send_sem, recv_sem):
        q = peer(k)
        return pltpu.make_async_remote_copy(
            src_ref=src.at[q],
            dst_ref=dst.at[chip],
            send_sem=send_sem.at[k],
            recv_sem=recv_sem.at[k],
            device_id=(z, q * 2 + core),
            device_id_type=MESH,
        )

    def expert_v(k):
        return to_expert(k, send_v, recv_v, sv_sem, rv_sem)

    def expert_s(k):
        return to_expert(k, send_s, recv_s, ss_sem, rs_sem)

    def expert_f(k):
        return to_expert(k, send_f, recv_f, sf_sem, rf_sem)

    keep_v, keep_s, keep_f = (
        pltpu.make_async_copy(src.at[chip], dst.at[chip], own_sem.at[i])
        for i, (src, dst) in enumerate(((send_v, recv_v), (send_s, recv_s), (send_f, recv_f)))
    )

    small[0].wait()
    key_f, hot_f, first_f, second_f = routing(fids[...], GROUPS_F)
    for copy in loads[0]:
        copy.wait()
    fill(send_f, 0, dot(hot_f[:, : 2 * TOK], half_x[0]))
    fill(send_f, HALF, dot(hot_f[:, 2 * TOK : 2 * TOK + PIECES * TOK], piece_x[...]))
    pl.semaphore_wait(barrier, CHIPS + (z + last - 1) // last + z // last)

    for k in FAR_FIRST:
        expert_f(k).start()
    keep_f.start()

    exchange = [
        pltpu.make_async_remote_copy(
            src_ref=src,
            dst_ref=dst.at[1],
            send_sem=wx_send.at[i],
            recv_sem=wx_recv.at[i],
            device_id=(z, sibling),
            device_id_type=MESH,
        )
        for i, (src, dst) in enumerate(((gate, wg), (up, wu), (down, wd)))
    ]
    for copy in weights + exchange + bases:
        copy.start()

    @pl.when(z > 0)
    def _():
        pl.semaphore_signal(ready.at[0], inc=1, device_id=(below, me), device_id_type=MESH)

    @pl.when(z == last)
    def _():
        pl.semaphore_signal(ready.at[1], inc=1, device_id=(above, me), device_id_type=MESH)

    for copy in small[1:] + loads[1] + loads[2]:
        copy.wait()
    key_b, hot_b, first_b, second_b = routing(bids[...], GROUPS_B)
    scale_m, scale_r = slot_gates(key_b, first_b, second_b, bgates[...])
    joint_v = hot_b[:, GROUPS_F * TOK : (GROUPS_F + JOINT) * TOK]
    joint_s = hot_b[:, (GROUPS_F + JOINT) * TOK :]
    fill(send_v, 0, dot(hot_b[:, : 2 * TOK], half_x[1]))
    fill(send_v, HALF, dot(joint_v, joint_x[0]) + dot(joint_s, joint_x[1]) * scale_r)
    for k in FAR_FIRST:
        expert_f(k).wait_send()
        expert_v(k).start()
    keep_v.start()
    fill(send_s, 0, dot(hot_b[:, : 2 * TOK], half_x[2]) * scale_m)

    def flip(hot):
        n = hot.shape[1]
        unit = as_hot(iota((n, n), 0) == iota((n, n), 1))
        return dot_nt(unit, hot).astype(BF16)

    hot_m[0] = flip(hot_b[:, : 2 * TOK])
    hot_r[0] = flip(hot_b[:, 2 * TOK : GROUPS_F * TOK])
    scale_m, scale_r = slot_gates(key_f, first_f, second_f, fgates[...])
    high_m, high_r = scale_m.astype(BF16).astype(F32), scale_r.astype(BF16).astype(F32)
    hot_main, hot_rest = hot_f[:, : 2 * TOK].astype(F32), hot_f[:, 2 * TOK :].astype(F32)
    hot_m[1] = flip((hot_main * high_m).astype(BF16))
    hot_r[1] = flip((hot_rest * high_r).astype(BF16))
    hot_m[2] = flip((hot_main * (scale_m - high_m)).astype(BF16))
    hot_r[2] = flip((hot_rest * (scale_r - high_r)).astype(BF16))
    for k in FAR_FIRST:
        expert_v(k).wait_send()
        expert_s(k).start()
    keep_s.start()

    def unpack(src, dst):
        def step(i, carry):
            pair = src[pl.ds(2 * i, 2), :, :HALF].astype(F32)
            halves = pair.reshape(2, 2, 8, HALF)
            rows = pl.ds(pl.multiple_of(16 * i, 16), 16)
            dst[rows, :HALF] = halves[:, 0].reshape(16, HALF).astype(BF16)
            dst[rows, HALF:] = halves[:, 1].reshape(16, HALF).astype(BF16)
            return carry

        lax.fori_loop(0, CHIPS // 2, step, 0)

    def unit_of(u):
        return u // 2, pl.ds(pl.multiple_of(lax.rem(u, 2) * BLOCK, BLOCK), BLOCK)

    def act_of(u):
        return pl.ds(pl.multiple_of(u * BLOCK, BLOCK), BLOCK)

    def to_token(k, c, width, src, dst, send_sem, recv_sem):
        q = peer(k)
        return pltpu.make_async_remote_copy(
            src_ref=src.at[c, q, :, pl.ds(0, width)],
            dst_ref=dst.at[c, chip, :, pl.ds(0, width)],
            send_sem=send_sem.at[c],
            recv_sem=recv_sem.at[c],
            device_id=(z, q * 2 + core),
            device_id_type=MESH,
        )

    def emit(column, c, steps, ret):
        lows = [column(2 * c + i) for i in range(steps)]
        highs = [column(2 * c + i + 7) for i in range(steps)]
        for i in range(steps):
            main = jnp.concatenate(
                [y[:128].reshape(CHIPS, 8, BLOCK) for y in (lows[i], highs[i])], axis=1
            )
            ret[c, :, :, i * BLOCK : (i + 1) * BLOCK] = main.astype(BF16)
        rests = [
            y[128:, j * LANES : (j + 1) * LANES] for y in lows + highs for j in range(BLOCK // LANES)
        ]
        n = len(rests) * 32
        order = as_hot(place(iota((MSG, n), 1), iota((MSG, n), 0)))
        rest = dot(order, jnp.concatenate(rests, axis=0).astype(BF16))
        wide = steps * BLOCK
        ret[c, :, :, wide : wide + LANES] = rest.astype(BF16).reshape(CHIPS, 16, LANES)

    def keep(c, wide, ret, got, recv_sem):
        return pltpu.make_async_copy(
            ret.at[c, chip, :, pl.ds(0, wide + LANES)],
            got.at[c, chip, :, pl.ds(0, wide + LANES)],
            recv_sem.at[c],
        )

    widths = (2 * BLOCK,) * (CHUNKS - 1) + (BLOCK,)

    def hidden_ab(u, carry):
        j, cols = unit_of(u)
        pre_a[u] = dot(rows_v[...], wg[j, :, cols])
        pre_b[u] = dot(rows_v[...], wu[j, :, cols])
        return carry

    def hidden_f(u, carry):
        j, cols = unit_of(u)
        a = dot(rows_f[...], wg[j, :, cols])
        b = dot(rows_f[...], wu[j, :, cols])
        act_a[:, act_of(u)] = (a * jax.nn.sigmoid(a) * b).astype(BF16)
        return carry

    def hidden_b(u, carry):
        j, cols = unit_of(u)
        a, b = pre_a[u], pre_b[u]
        dh = dot_nt(rows_s[...], wd[j, cols, :])
        sig = jax.nn.sigmoid(a)
        act_a[:, act_of(u)] = (dh * b * sig * (1.0 + a * (1.0 - sig))).astype(BF16)
        act_b[:, act_of(u)] = (dh * (a * sig)).astype(BF16)
        return carry

    def column_f(n):
        cols = pl.ds(pl.multiple_of(n * BLOCK, BLOCK), BLOCK)
        total = jnp.zeros((ROWS, BLOCK), F32)
        for j in range(2):
            total += dot(act_a[:, j * UNIT : (j + 1) * UNIT], wd[j, :, cols])
        return total

    def column_b(n):
        rows = pl.ds(pl.multiple_of(n * BLOCK, BLOCK), BLOCK)
        total = jnp.zeros((ROWS, BLOCK), F32)
        for j in range(2):
            total += dot_nt(act_a[:, j * UNIT : (j + 1) * UNIT], wg[j, rows, :])
            total += dot_nt(act_b[:, j * UNIT : (j + 1) * UNIT], wu[j, rows, :])
        return total

    def return_f(k, c):
        return to_token(k, c, widths[c] + LANES, ret_f, got_f, tf_send, tf_recv)

    for k in FAR_FIRST:
        expert_f(k).wait_recv()
    keep_f.wait()
    unpack(recv_f, rows_f)
    n = PIECES * 32
    order = as_hot(place(iota((n, MSG), 0), iota((n, MSG), 1)))
    plain = dot(order, recv_f[:, :, HALF:].reshape(MSG, PIECE)).astype(BF16)
    for k in range(PIECES):
        rows_f[128:ROWS, k * PIECE : (k + 1) * PIECE] = plain[32 * k : 32 * k + 32]
    for copy in weights:
        copy.wait()
    lax.fori_loop(0, 2, hidden_f, 0)
    for copy in exchange:
        copy.wait_recv()
    lax.fori_loop(2, 4, hidden_f, 0)

    def step_f(c, carry):
        emit(column_f, c, 2, ret_f)
        return carry

    lax.fori_loop(0, CHUNKS - 1, step_f, 0)
    emit(column_f, CHUNKS - 1, 1, ret_f)

    for k in FAR_FIRST:
        expert_v(k).wait_recv()
    keep_v.wait()
    unpack(recv_v, rows_v)
    order = as_hot(place_joint(iota((MSG, MSG), 0), iota((MSG, MSG), 1)))
    plain = dot(order, recv_v[:, :, HALF:].reshape(MSG, JOINT_PIECE)).astype(BF16)
    for k in range(JOINT):
        cols = slice(k * JOINT_PIECE, (k + 1) * JOINT_PIECE)
        rows_v[128:ROWS, cols] = plain[64 * k : 64 * k + 32]
        rows_s[128:ROWS, cols] = plain[64 * k + 32 : 64 * k + 64]
    lax.fori_loop(0, 4, hidden_ab, 0)
    for k in FAR_FIRST:
        expert_s(k).wait_send()
        for c in range(EARLY):
            return_f(k, c).start()
    for c in range(EARLY):
        keep(c, widths[c], ret_f, got_f, tf_recv).start()

    def late_f():
        for c in range(EARLY, CHUNKS):
            for k in FAR_FIRST:
                return_f(k, c).start()
            keep(c, widths[c], ret_f, got_f, tf_recv).start()

    pl.when(jnp.logical_not(upward))(late_f)
    for k in FAR_FIRST:
        expert_s(k).wait_recv()
    keep_s.wait()
    unpack(recv_s, rows_s)
    lax.fori_loop(0, 4, hidden_b, 0)

    def send_back(c, wide):
        for k in FAR_FIRST:
            to_token(k, c, wide + LANES, ret_b, got_b, tb_send, tb_recv).start()
        keep(c, wide, ret_b, got_b, tb_recv).start()

    def step_b(c, carry):
        emit(column_b, c, 2, ret_b)
        send_back(c, 2 * BLOCK)
        return carry

    lax.fori_loop(0, CHUNKS - 1, step_b, 0)
    emit(column_b, CHUNKS - 1, 1, ret_b)
    send_back(CHUNKS - 1, BLOCK)

    pl.when(upward)(late_f)

    def hop(c, h, wide, src, dst, section, send_sem, recv_sem):
        cols = pl.ds(h * HALF + 2 * BLOCK * c, wide)
        return pltpu.make_async_remote_copy(
            src_ref=src.at[:, cols],
            dst_ref=dst.at[:, cols],
            send_sem=send_sem.at[2 * c + h],
            recv_sem=recv_sem.at[2 * c + h],
            device_id=(section, me),
            device_id_type=MESH,
        )

    def hops(src, dst, section, send_sem, recv_sem):
        return [
            hop(c, h, 2 * BLOCK if c < CHUNKS - 1 else BLOCK, src, dst, section, send_sem, recv_sem)
            for c in range(CHUNKS)
            for h in range(2)
        ]

    def combine(got, recv_sem, kinds, base, total, moves, chunks):
        for c in chunks:
            wide = 2 * BLOCK if c < CHUNKS - 1 else BLOCK
            here = got.at[c, :, :, pl.ds(0, wide + LANES)]
            pltpu.make_async_copy(here, here, recv_sem.at[c]).wait()
            pieces = wide // LANES
            rows = got[c, :, :, :wide].reshape(MSG, wide)
            tail = got[c, :, :, wide : wide + LANES].reshape(MSG, LANES)
            main = sum(dot(hot_m[i], rows) for i in kinds)
            rest = sum(dot(hot_r[i, : 2 * pieces * TOK], tail) for i in kinds)
            for h in range(2):
                for i in range(pieces):
                    at = h * HALF + 2 * BLOCK * c + i * LANES
                    k = h * pieces + i
                    total[:, at : at + LANES] = (
                        base[:, at : at + LANES].astype(F32)
                        + main[h * TOK : (h + 1) * TOK, i * LANES : (i + 1) * LANES]
                        + rest[k * TOK : (k + 1) * TOK]
                    ).astype(BF16)
                moves[2 * c + h].start()

    moves_b = hops(sum_b, out.at[1], below, hb_send, hb_recv)
    moves_f = hops(sum_f, out.at[0], above, hf_send, hf_recv)
    for copy in bases:
        copy.wait()

    @pl.when(z < last)
    def _():
        pl.semaphore_wait(ready.at[0], 1)

    @pl.when(z == 0)
    def _():
        pl.semaphore_wait(ready.at[1], 1)

    def combine_f(chunks):
        combine(got_f, tf_recv, (1, 2), base_x, sum_f, moves_f, chunks)

    combine_f(range(EARLY))
    pl.when(jnp.logical_not(upward))(lambda: combine_f(range(EARLY, CHUNKS)))
    combine(got_b, tb_recv, (0,), base_c, sum_b, moves_b, range(CHUNKS))
    pl.when(upward)(lambda: combine_f(range(EARLY, CHUNKS)))

    for copy in exchange:
        copy.wait_send()
    for ret, send_sem in ((ret_b, tb_send), (ret_f, tf_send)):
        for c in range(CHUNKS):
            wide = 2 * BLOCK if c < CHUNKS - 1 else BLOCK
            sent = ret.at[c, pl.ds(0, CHIPS - 1), :, pl.ds(0, wide + LANES)]
            pltpu.make_async_copy(sent, sent, send_sem.at[c]).wait()
    for copy in moves_b + moves_f:
        copy.wait()


def body(
    fwd_input, fwd_experts, fwd_gates, bwd_input, bwd_cotangent, bwd_experts, bwd_gates,
    w_gate, w_up, w_down,
):
    vmem, anywhere = pl.BlockSpec(memory_space=pltpu.VMEM), pl.BlockSpec(memory_space=pl.ANY)
    rows = pltpu.VMEM((TOK, D), BF16)
    messages = pltpu.VMEM((CHIPS, 16, WIDE), BF16)
    joint = pltpu.VMEM((CHIPS, 16, HALF + JOINT_PIECE), BF16)
    halves = pltpu.VMEM((CHIPS, 16, HALF), BF16)
    chunks = pltpu.VMEM((CHUNKS, CHIPS, 16, CHUNK), BF16)
    dma = pltpu.SemaphoreType.DMA
    out = pl.pallas_call(
        kernel,
        out_shape=pltpu.VMEM((2, TOK, D), BF16),
        in_specs=[anywhere] * 10,
        out_specs=vmem,
        scratch_shapes=[
            pltpu.VMEM((2, TOK), jnp.int32),
            pltpu.VMEM((2, TOK), F32),
            pltpu.VMEM((2, TOK), jnp.int32),
            pltpu.VMEM((2, TOK), F32),
            pltpu.VMEM((3, 2 * TOK, HALF), BF16),
            pltpu.VMEM((PIECES * TOK, PIECE), BF16),
            pltpu.VMEM((2, JOINT * TOK, JOINT_PIECE), BF16),
        ]
        + [joint, halves, messages] * 2
        + [chunks] * 4
        + [
            pltpu.VMEM((2, D, UNIT), BF16),
            pltpu.VMEM((2, D, UNIT), BF16),
            pltpu.VMEM((2, UNIT, D), BF16),
            pltpu.VMEM((ROWS, D), BF16),
            pltpu.VMEM((ROWS, D), BF16),
            pltpu.VMEM((ROWS, D), BF16),
            pltpu.VMEM((4, ROWS, BLOCK), F32),
            pltpu.VMEM((4, ROWS, BLOCK), F32),
            pltpu.VMEM((ROWS, 2 * UNIT), BF16),
            pltpu.VMEM((ROWS, 2 * UNIT), BF16),
            rows, rows, rows, rows,
            pltpu.VMEM((3, 2 * TOK, MSG), BF16),
            pltpu.VMEM((3, 8 * TOK, MSG), BF16),
            dma((4,)), dma((6,)), dma((2 * JOINT + PIECES,)), dma((2,)), dma((3,)), dma((3,)), dma((3,)), dma((3,)),
        ]
        + [dma((CHIPS,))] * 6
        + [dma((CHUNKS,))] * 4
        + [dma((2 * CHUNKS,))] * 4
        + [pltpu.SemaphoreType.REGULAR((2,))],
        compiler_params=pltpu.CompilerParams(
            collective_id=0, has_side_effects=True, vmem_limit_bytes=60 << 20
        ),
        name="relay_experts",
    )(
        fwd_experts[0].T, fwd_gates[0].T, bwd_experts[0].T, bwd_gates[0].T,
        fwd_input[0], bwd_input[0], bwd_cotangent[0], w_gate[0], w_up[0], w_down[0],
    )
    return out[0:1], out[1:2]


def solution(mesh):
    tokens = P("pp", "ep", None)
    in_specs = (tokens,) * 7 + (P("pp", None, "ep"), P("pp", None, "ep"), tokens)
    return jax.shard_map(
        body, mesh=mesh, in_specs=in_specs, out_specs=(tokens, tokens), check_vma=False
    )
```

```python
import jax
import jax.numpy as jnp
from jax import lax
from jax.experimental import pallas as pl
from jax.experimental.pallas import tpu as pltpu
from jax.sharding import PartitionSpec as P

MESH = pl.DeviceIdType.MESH
F32 = jnp.float32
BF16 = jnp.bfloat16

D = 3584
UNIT = 512
TOK = 64
CHIPS = 16
SIDE = 4
ROWS = 160
HALF = D // 2
PIECE = 512
PIECES = D // PIECE
WIDE = HALF + PIECE
MSG = CHIPS * 16
BLOCK = 256
LANES = 128
CHUNKS = 4
EARLY = 2
CHUNK = 2 * BLOCK + LANES
JOINT = 4
JOINT_PIECE = D // JOINT
GROUPS_F = 2 + 8
GROUPS_B = GROUPS_F + 2 * JOINT
FAR_FIRST = (10, 9, 14, 11, 6, 5, 13, 15, 7, 8, 2, 4, 1, 12, 3)


def dot(a, b):
    return lax.dot_general(a, b, (((1,), (0,)), ((), ())), preferred_element_type=F32)


def dot_nt(a, b):
    return lax.dot_general(a, b, (((1,), (1,)), ((), ())), preferred_element_type=F32)


def iota(shape, dim):
    return lax.broadcasted_iota(jnp.int32, shape, dim)


def as_hot(mask):
    return jnp.where(mask, 1.0, 0.0).astype(BF16)


def routing(ids, groups):
    expert = iota((CHIPS, TOK), 0)
    first, second = ids[0:1, :] == expert, ids[1:2, :] == expert
    hits = jnp.where(first | second, 1.0, 0.0)
    before = as_hot(iota((TOK, TOK), 0) < iota((TOK, TOK), 1))
    keys = hits * (dot(hits.astype(BF16), before) + 1.0)
    hots = groups * TOK
    copies = as_hot((iota((TOK, hots), 1) & (TOK - 1)) == iota((TOK, hots), 0))
    wide = dot(keys.astype(BF16), copies).astype(BF16)
    key = dot(rows_of_expert(BF16), wide)
    slot = iota((MSG, hots), 0) & 15
    group = iota((MSG, hots), 1) >> 6
    first_slot = (group - 2) * 2
    if groups > GROUPS_F:
        joint = group - GROUPS_F
        joint = jnp.where(joint < JOINT, joint * 4, (joint - JOINT) * 4 + 2)
        first_slot = jnp.where(group < GROUPS_F, first_slot, joint)
    want_main = (slot - 8 * group).astype(F32)
    want_rest = (slot - first_slot).astype(F32)
    main = (want_main >= 0.0) & (want_main < 8.0) & (key == want_main + 1.0)
    rest = (want_rest >= 0.0) & (want_rest < 2.0) & (key == want_rest + 9.0)
    hot = as_hot(main | rest)
    return key[:, :TOK], hot, first, second


def rows_of_expert(dtype):
    row, expert = iota((MSG, CHIPS), 0), iota((MSG, CHIPS), 1)
    return jnp.where((row >> 4) == expert, 1.0, 0.0).astype(dtype)


def slot_gates(key, first, second, gates):
    per = jnp.where(first, gates[0:1, :], 0.0) + jnp.where(second, gates[1:2, :], 0.0)
    spread = lax.dot_general(
        rows_of_expert(F32),
        per,
        (((1,), (0,)), ((), ())),
        precision=lax.Precision.HIGHEST,
        preferred_element_type=F32,
    )
    slot = iota((MSG, TOK), 0)
    main = key == (slot & 7).astype(F32) + 1.0
    rest = key == (slot & 1).astype(F32) + 9.0
    return (
        jnp.sum(jnp.where(main, spread, 0.0), axis=1, keepdims=True),
        jnp.sum(jnp.where(rest, spread, 0.0), axis=1, keepdims=True),
    )


def place(u, v):
    return (((u >> 1) & 15) << 4) + ((u >> 5) << 1) + (u & 1) == v


def place_joint(u, v):
    return (((u >> 1) & 15) << 4) + ((u >> 6) << 2) + (((u >> 5) & 1) << 1) + (u & 1) == v


def kernel(
    fids_in, fgates_in, bids_in, bgates_in, xf, xb, cb, gate, up, down,
    out,
    fids, fgates, bids, bgates, half_x, piece_x, joint_x, send_v, send_s, send_f, recv_v, recv_s, recv_f, ret_b, ret_f, got_b, got_f,
    wg, wu, wd, rows_f, rows_v, rows_s, pre_a, pre_b, act_a, act_b,
    base_x, base_c, sum_f, sum_b, left_f, hot_m, hot_r,
    small_sem, in_sem, joint_sem, base_sem, w_sem, own_sem, wx_send, wx_recv,
    sv_sem, rv_sem, ss_sem, rs_sem, sf_sem, rf_sem,
    tb_send, tb_recv, tf_send, tf_recv, hb_send, hb_recv, hf_send, hf_recv, ready,
):
    z, me = lax.axis_index("pp"), lax.axis_index("ep")
    sections = lax.axis_size("pp")
    chip, core = me // 2, lax.rem(me, 2)
    above, below = lax.rem(z + 1, sections), lax.rem(z + sections - 1, sections)
    last = sections - 1
    upward = z < last
    sibling = chip * 2 + 1 - core

    def peer(k):
        x = lax.rem(chip // SIDE + k // SIDE, SIDE)
        y = lax.rem(lax.rem(chip, SIDE) + k % SIDE, SIDE)
        return x * SIDE + y

    small = [
        pltpu.make_async_copy(src, dst, small_sem.at[i])
        for i, (src, dst) in enumerate(
            ((fids_in, fids), (fgates_in, fgates), (bids_in, bids), (bgates_in, bgates))
        )
    ]
    loads = []
    for i, src in enumerate((xf, xb, cb)):
        own = [
            pltpu.make_async_copy(
                src.at[:, pl.ds(h * HALF, HALF)],
                half_x.at[i, pl.ds(h * TOK, TOK)],
                in_sem.at[i * 2 + h],
            )
            for h in range(2)
        ]
        pieces, width, at = (
            (piece_x, PIECE, 2 * JOINT)
            if i == 0
            else (joint_x.at[i - 1], JOINT_PIECE, (i - 1) * JOINT)
        )
        for k in range(D // width):
            own.append(
                pltpu.make_async_copy(
                    src.at[:, pl.ds(k * width, width)],
                    pieces.at[pl.ds(k * TOK, TOK)],
                    joint_sem.at[at + k],
                )
            )
        loads.append(own)
    barrier = pltpu.get_barrier_semaphore()
    for k in FAR_FIRST:
        pl.semaphore_signal(
            barrier, inc=1, device_id=(z, peer(k) * 2 + core), device_id_type=MESH
        )
    pl.semaphore_signal(barrier, inc=1, device_id=(z, sibling), device_id_type=MESH)

    @pl.when(z < last)
    def _():
        pl.semaphore_signal(barrier, inc=1, device_id=(above, me), device_id_type=MESH)

    @pl.when(z == 0)
    def _():
        pl.semaphore_signal(barrier, inc=1, device_id=(below, me), device_id_type=MESH)


    for copy in small[:1] + loads[0]:
        copy.start()
    for copy in small[1:] + loads[1] + loads[2]:
        copy.start()

    weights = [
        pltpu.make_async_copy(src, dst.at[0], w_sem.at[i])
        for i, (src, dst) in enumerate(((gate, wg), (up, wu), (down, wd)))
    ]
    bases = [
        pltpu.make_async_copy(xf, base_x, base_sem.at[0]),
        pltpu.make_async_copy(cb, base_c, base_sem.at[1]),
    ]

    def fill(dst, at, rows):
        width = rows.shape[1]
        dst[:, :, at : at + width] = rows.astype(BF16).reshape(CHIPS, 16, width)

    def to_expert(k, src, dst, send_sem, recv_sem):
        q = peer(k)
        return pltpu.make_async_remote_copy(
            src_ref=src.at[q],
            dst_ref=dst.at[chip],
            send_sem=send_sem.at[k],
            recv_sem=recv_sem.at[k],
            device_id=(z, q * 2 + core),
            device_id_type=MESH,
        )

    def expert_v(k):
        return to_expert(k, send_v, recv_v, sv_sem, rv_sem)

    def expert_s(k):
        return to_expert(k, send_s, recv_s, ss_sem, rs_sem)

    def expert_f(k):
        return to_expert(k, send_f, recv_f, sf_sem, rf_sem)

    keep_v, keep_s, keep_f = (
        pltpu.make_async_copy(src.at[chip], dst.at[chip], own_sem.at[i])
        for i, (src, dst) in enumerate(((send_v, recv_v), (send_s, recv_s), (send_f, recv_f)))
    )

    small[0].wait()
    key_f, hot_f, first_f, second_f = routing(fids[...], GROUPS_F)
    for copy in loads[0]:
        copy.wait()
    fill(send_f, 0, dot(hot_f[:, : 2 * TOK], half_x[0]))
    fill(send_f, HALF, dot(hot_f[:, 2 * TOK : 2 * TOK + PIECES * TOK], piece_x[...]))
    pl.semaphore_wait(barrier, CHIPS + (z + last - 1) // last + z // last)

    for k in FAR_FIRST:
        expert_f(k).start()
    keep_f.start()

    exchange = [
        pltpu.make_async_remote_copy(
            src_ref=src,
            dst_ref=dst.at[1],
            send_sem=wx_send.at[i],
            recv_sem=wx_recv.at[i],
            device_id=(z, sibling),
            device_id_type=MESH,
        )
        for i, (src, dst) in enumerate(((gate, wg), (up, wu), (down, wd)))
    ]
    for copy in weights + exchange + bases:
        copy.start()

    @pl.when(z > 0)
    def _():
        pl.semaphore_signal(ready.at[0], inc=1, device_id=(below, me), device_id_type=MESH)

    @pl.when(z == last)
    def _():
        pl.semaphore_signal(ready.at[1], inc=1, device_id=(above, me), device_id_type=MESH)

    for copy in small[1:] + loads[1] + loads[2]:
        copy.wait()
    key_b, hot_b, first_b, second_b = routing(bids[...], GROUPS_B)
    scale_m, scale_r = slot_gates(key_b, first_b, second_b, bgates[...])
    joint_v = hot_b[:, GROUPS_F * TOK : (GROUPS_F + JOINT) * TOK]
    joint_s = hot_b[:, (GROUPS_F + JOINT) * TOK :]
    fill(send_v, 0, dot(hot_b[:, : 2 * TOK], half_x[1]))
    fill(send_v, HALF, dot(joint_v, joint_x[0]) + dot(joint_s, joint_x[1]) * scale_r)
    for k in FAR_FIRST:
        expert_f(k).wait_send()
        expert_v(k).start()
    keep_v.start()
    fill(send_s, 0, dot(hot_b[:, : 2 * TOK], half_x[2]) * scale_m)

    def flip(hot):
        n = hot.shape[1]
        unit = as_hot(iota((n, n), 0) == iota((n, n), 1))
        return dot_nt(unit, hot).astype(BF16)

    hot_m[0] = flip(hot_b[:, : 2 * TOK])
    hot_r[0] = flip(hot_b[:, 2 * TOK : GROUPS_F * TOK])
    scale_m, scale_r = slot_gates(key_f, first_f, second_f, fgates[...])
    high_m, high_r = scale_m.astype(BF16).astype(F32), scale_r.astype(BF16).astype(F32)
    hot_main, hot_rest = hot_f[:, : 2 * TOK].astype(F32), hot_f[:, 2 * TOK :].astype(F32)
    hot_m[1] = flip((hot_main * high_m).astype(BF16))
    hot_r[1] = flip((hot_rest * high_r).astype(BF16))
    hot_m[2] = flip((hot_main * (scale_m - high_m)).astype(BF16))
    hot_r[2] = flip((hot_rest * (scale_r - high_r)).astype(BF16))
    for k in FAR_FIRST:
        expert_v(k).wait_send()
        expert_s(k).start()
    keep_s.start()

    def unpack(src, dst):
        def step(i, carry):
            pair = src[pl.ds(2 * i, 2), :, :HALF].astype(F32)
            halves = pair.reshape(2, 2, 8, HALF)
            rows = pl.ds(pl.multiple_of(16 * i, 16), 16)
            dst[rows, :HALF] = halves[:, 0].reshape(16, HALF).astype(BF16)
            dst[rows, HALF:] = halves[:, 1].reshape(16, HALF).astype(BF16)
            return carry

        lax.fori_loop(0, CHIPS // 2, step, 0)

    def unit_of(u):
        return u // 2, pl.ds(pl.multiple_of(lax.rem(u, 2) * BLOCK, BLOCK), BLOCK)

    def act_of(u):
        return pl.ds(pl.multiple_of(u * BLOCK, BLOCK), BLOCK)

    def to_token(k, c, width, src, dst, send_sem, recv_sem):
        q = peer(k)
        return pltpu.make_async_remote_copy(
            src_ref=src.at[c, q, :, pl.ds(0, width)],
            dst_ref=dst.at[c, chip, :, pl.ds(0, width)],
            send_sem=send_sem.at[c],
            recv_sem=recv_sem.at[c],
            device_id=(z, q * 2 + core),
            device_id_type=MESH,
        )

    def emit(column, c, steps, ret, hold=None, extra=None):
        lows = [column(2 * c + i) for i in range(steps)]
        highs = [column(2 * c + i + 7) for i in range(steps)]
        for i in range(steps):
            main = jnp.concatenate(
                [y[:128].reshape(CHIPS, 8, BLOCK) for y in (lows[i], highs[i])], axis=1
            )
            ret[c, :, :, i * BLOCK : (i + 1) * BLOCK] = main.astype(BF16)
        rests = [
            y[128:, j * LANES : (j + 1) * LANES] for y in lows + highs for j in range(BLOCK // LANES)
        ]
        stacked = jnp.concatenate(rests, axis=0).astype(BF16)
        if hold is not None:
            hold[...] = stacked
        if extra is not None:
            stacked = jnp.concatenate([stacked, extra[...]], axis=0)
        n = stacked.shape[0]
        order = as_hot(place(iota((MSG, n), 1), iota((MSG, n), 0)))
        rest = dot(order, stacked)
        wide = steps * BLOCK
        ret[c, :, :, wide : wide + LANES] = rest.astype(BF16).reshape(CHIPS, 16, LANES)

    def keep(c, width, ret, got, recv_sem):
        return pltpu.make_async_copy(
            ret.at[c, chip, :, pl.ds(0, width)],
            got.at[c, chip, :, pl.ds(0, width)],
            recv_sem.at[c],
        )

    widths = (2 * BLOCK,) * (CHUNKS - 1) + (BLOCK,)

    def hidden_ab(u, carry):
        j, cols = unit_of(u)
        pre_a[u] = dot(rows_v[...], wg[j, :, cols])
        pre_b[u] = dot(rows_v[...], wu[j, :, cols])
        return carry

    def hidden_f(u, carry):
        j, cols = unit_of(u)
        a = dot(rows_f[...], wg[j, :, cols])
        b = dot(rows_f[...], wu[j, :, cols])
        act_a[:, act_of(u)] = (a * jax.nn.sigmoid(a) * b).astype(BF16)
        return carry

    def hidden_b(u, carry):
        j, cols = unit_of(u)
        a, b = pre_a[u], pre_b[u]
        dh = dot_nt(rows_s[...], wd[j, cols, :])
        sig = jax.nn.sigmoid(a)
        act_a[:, act_of(u)] = (dh * b * sig * (1.0 + a * (1.0 - sig))).astype(BF16)
        act_b[:, act_of(u)] = (dh * (a * sig)).astype(BF16)
        return carry

    def column_f(n):
        cols = pl.ds(pl.multiple_of(n * BLOCK, BLOCK), BLOCK)
        total = jnp.zeros((ROWS, BLOCK), F32)
        for j in range(2):
            total += dot(act_a[:, j * UNIT : (j + 1) * UNIT], wd[j, :, cols])
        return total

    def column_b(n):
        rows = pl.ds(pl.multiple_of(n * BLOCK, BLOCK), BLOCK)
        total = jnp.zeros((ROWS, BLOCK), F32)
        for j in range(2):
            total += dot_nt(act_a[:, j * UNIT : (j + 1) * UNIT], wg[j, rows, :])
            total += dot_nt(act_b[:, j * UNIT : (j + 1) * UNIT], wu[j, rows, :])
        return total

    def width_f(c, shared):
        return widths[c] + (0 if shared and c == CHUNKS - 1 else LANES)

    def return_f(k, c, shared):
        return to_token(k, c, width_f(c, shared), ret_f, got_f, tf_send, tf_recv)

    for k in FAR_FIRST:
        expert_f(k).wait_recv()
    keep_f.wait()
    unpack(recv_f, rows_f)
    n = PIECES * 32
    order = as_hot(place(iota((n, MSG), 0), iota((n, MSG), 1)))
    plain = dot(order, recv_f[:, :, HALF:].reshape(MSG, PIECE)).astype(BF16)
    for k in range(PIECES):
        rows_f[128:ROWS, k * PIECE : (k + 1) * PIECE] = plain[32 * k : 32 * k + 32]
    for copy in weights:
        copy.wait()
    lax.fori_loop(0, 2, hidden_f, 0)
    for copy in exchange:
        copy.wait_recv()
    lax.fori_loop(2, 4, hidden_f, 0)

    def step_f(c, carry):
        emit(column_f, c, 2, ret_f)
        return carry

    lax.fori_loop(0, CHUNKS - 1, step_f, 0)
    emit(column_f, CHUNKS - 1, 1, ret_f, hold=left_f)

    for k in FAR_FIRST:
        expert_v(k).wait_recv()
    keep_v.wait()
    unpack(recv_v, rows_v)
    order = as_hot(place_joint(iota((MSG, MSG), 0), iota((MSG, MSG), 1)))
    plain = dot(order, recv_v[:, :, HALF:].reshape(MSG, JOINT_PIECE)).astype(BF16)
    for k in range(JOINT):
        cols = slice(k * JOINT_PIECE, (k + 1) * JOINT_PIECE)
        rows_v[128:ROWS, cols] = plain[64 * k : 64 * k + 32]
        rows_s[128:ROWS, cols] = plain[64 * k + 32 : 64 * k + 64]
    lax.fori_loop(0, 4, hidden_ab, 0)
    for k in FAR_FIRST:
        expert_s(k).wait_send()
        for c in range(EARLY):
            return_f(k, c, False).start()
    for c in range(EARLY):
        keep(c, width_f(c, False), ret_f, got_f, tf_recv).start()

    def late_f(shared):
        for c in range(EARLY, CHUNKS):
            for k in FAR_FIRST:
                return_f(k, c, shared).start()
            keep(c, width_f(c, shared), ret_f, got_f, tf_recv).start()

    pl.when(jnp.logical_not(upward))(lambda: late_f(False))
    for k in FAR_FIRST:
        expert_s(k).wait_recv()
    keep_s.wait()
    unpack(recv_s, rows_s)
    lax.fori_loop(0, 4, hidden_b, 0)

    def send_back(c, wide):
        for k in FAR_FIRST:
            to_token(k, c, wide + LANES, ret_b, got_b, tb_send, tb_recv).start()
        keep(c, wide + LANES, ret_b, got_b, tb_recv).start()

    def step_b(c, carry):
        emit(column_b, c, 2, ret_b)
        send_back(c, 2 * BLOCK)
        return carry

    lax.fori_loop(0, CHUNKS - 1, step_b, 0)
    emit(column_b, CHUNKS - 1, 1, ret_b, extra=left_f)
    send_back(CHUNKS - 1, BLOCK)

    pl.when(upward)(lambda: late_f(True))

    def hop(c, h, wide, src, dst, section, send_sem, recv_sem):
        cols = pl.ds(h * HALF + 2 * BLOCK * c, wide)
        return pltpu.make_async_remote_copy(
            src_ref=src.at[:, cols],
            dst_ref=dst.at[:, cols],
            send_sem=send_sem.at[2 * c + h],
            recv_sem=recv_sem.at[2 * c + h],
            device_id=(section, me),
            device_id_type=MESH,
        )

    def hops(src, dst, section, send_sem, recv_sem):
        return [
            hop(c, h, 2 * BLOCK if c < CHUNKS - 1 else BLOCK, src, dst, section, send_sem, recv_sem)
            for c in range(CHUNKS)
            for h in range(2)
        ]

    def combine(got, recv_sem, kinds, base, total, moves, chunks, shared=None):
        for c in chunks:
            wide = 2 * BLOCK if c < CHUNKS - 1 else BLOCK
            elsewhere = shared is not None and c == CHUNKS - 1
            here = got.at[c, :, :, pl.ds(0, wide if elsewhere else wide + LANES)]
            pltpu.make_async_copy(here, here, recv_sem.at[c]).wait()
            pieces = wide // LANES
            rows = got[c, :, :, :wide].reshape(MSG, wide)
            tail = (shared if elsewhere else got)[c, :, :, wide : wide + LANES].reshape(MSG, LANES)
            first = 2 * pieces * TOK if elsewhere else 0
            main = sum(dot(hot_m[i], rows) for i in kinds)
            rest = sum(dot(hot_r[i, first : first + 2 * pieces * TOK], tail) for i in kinds)
            for h in range(2):
                for i in range(pieces):
                    at = h * HALF + 2 * BLOCK * c + i * LANES
                    k = h * pieces + i
                    total[:, at : at + LANES] = (
                        base[:, at : at + LANES].astype(F32)
                        + main[h * TOK : (h + 1) * TOK, i * LANES : (i + 1) * LANES]
                        + rest[k * TOK : (k + 1) * TOK]
                    ).astype(BF16)
                moves[2 * c + h].start()

    moves_b = hops(sum_b, out.at[1], below, hb_send, hb_recv)
    moves_f = hops(sum_f, out.at[0], above, hf_send, hf_recv)
    for copy in bases:
        copy.wait()

    @pl.when(z < last)
    def _():
        pl.semaphore_wait(ready.at[0], 1)

    @pl.when(z == 0)
    def _():
        pl.semaphore_wait(ready.at[1], 1)

    def combine_f(chunks, shared=None):
        combine(got_f, tf_recv, (1, 2), base_x, sum_f, moves_f, chunks, shared)

    combine_f(range(EARLY))
    pl.when(jnp.logical_not(upward))(lambda: combine_f(range(EARLY, CHUNKS)))
    combine(got_b, tb_recv, (0,), base_c, sum_b, moves_b, range(CHUNKS))
    pl.when(upward)(lambda: combine_f(range(EARLY, CHUNKS), got_b))

    for copy in exchange:
        copy.wait_send()

    def sent(ret, send_sem, c, width):
        part = ret.at[c, pl.ds(0, CHIPS - 1), :, pl.ds(0, width)]
        pltpu.make_async_copy(part, part, send_sem.at[c]).wait()

    for c in range(CHUNKS):
        sent(ret_b, tb_send, c, widths[c] + LANES)
    for c in range(CHUNKS - 1):
        sent(ret_f, tf_send, c, width_f(c, False))
    pl.when(upward)(lambda: sent(ret_f, tf_send, CHUNKS - 1, width_f(CHUNKS - 1, True)))
    pl.when(jnp.logical_not(upward))(
        lambda: sent(ret_f, tf_send, CHUNKS - 1, width_f(CHUNKS - 1, False))
    )
    for copy in moves_b + moves_f:
        copy.wait()


def body(
    fwd_input, fwd_experts, fwd_gates, bwd_input, bwd_cotangent, bwd_experts, bwd_gates,
    w_gate, w_up, w_down,
):
    vmem, anywhere = pl.BlockSpec(memory_space=pltpu.VMEM), pl.BlockSpec(memory_space=pl.ANY)
    rows = pltpu.VMEM((TOK, D), BF16)
    messages = pltpu.VMEM((CHIPS, 16, WIDE), BF16)
    joint = pltpu.VMEM((CHIPS, 16, HALF + JOINT_PIECE), BF16)
    halves = pltpu.VMEM((CHIPS, 16, HALF), BF16)
    chunks = pltpu.VMEM((CHUNKS, CHIPS, 16, CHUNK), BF16)
    dma = pltpu.SemaphoreType.DMA
    out = pl.pallas_call(
        kernel,
        out_shape=pltpu.VMEM((2, TOK, D), BF16),
        in_specs=[anywhere] * 10,
        out_specs=vmem,
        scratch_shapes=[
            pltpu.VMEM((2, TOK), jnp.int32),
            pltpu.VMEM((2, TOK), F32),
            pltpu.VMEM((2, TOK), jnp.int32),
            pltpu.VMEM((2, TOK), F32),
            pltpu.VMEM((3, 2 * TOK, HALF), BF16),
            pltpu.VMEM((PIECES * TOK, PIECE), BF16),
            pltpu.VMEM((2, JOINT * TOK, JOINT_PIECE), BF16),
        ]
        + [joint, halves, messages] * 2
        + [chunks] * 4
        + [
            pltpu.VMEM((2, D, UNIT), BF16),
            pltpu.VMEM((2, D, UNIT), BF16),
            pltpu.VMEM((2, UNIT, D), BF16),
            pltpu.VMEM((ROWS, D), BF16),
            pltpu.VMEM((ROWS, D), BF16),
            pltpu.VMEM((ROWS, D), BF16),
            pltpu.VMEM((4, ROWS, BLOCK), F32),
            pltpu.VMEM((4, ROWS, BLOCK), F32),
            pltpu.VMEM((ROWS, 2 * UNIT), BF16),
            pltpu.VMEM((ROWS, 2 * UNIT), BF16),
            rows, rows, rows, rows,
            pltpu.VMEM((4 * 32, LANES), BF16),
            pltpu.VMEM((3, 2 * TOK, MSG), BF16),
            pltpu.VMEM((3, 8 * TOK, MSG), BF16),
            dma((4,)), dma((6,)), dma((2 * JOINT + PIECES,)), dma((2,)), dma((3,)), dma((3,)), dma((3,)), dma((3,)),
        ]
        + [dma((CHIPS,))] * 6
        + [dma((CHUNKS,))] * 4
        + [dma((2 * CHUNKS,))] * 4
        + [pltpu.SemaphoreType.REGULAR((2,))],
        compiler_params=pltpu.CompilerParams(
            collective_id=0, has_side_effects=True, vmem_limit_bytes=60 << 20
        ),
        name="relay_experts",
    )(
        fwd_experts[0].T, fwd_gates[0].T, bwd_experts[0].T, bwd_gates[0].T,
        fwd_input[0], bwd_input[0], bwd_cotangent[0], w_gate[0], w_up[0], w_down[0],
    )
    return out[0:1], out[1:2]


def solution(mesh):
    tokens = P("pp", "ep", None)
    in_specs = (tokens,) * 7 + (P("pp", None, "ep"), P("pp", None, "ep"), tokens)
    return jax.shard_map(
        body, mesh=mesh, in_specs=in_specs, out_specs=(tokens, tokens), check_vma=False
    )
```
